256 devices in a mesh: section: 4 (over z_lo, core), shard: 64 (over y, z_hi, x).
Axes of the slice: x: 4, y: 4, z: 8 (z_hi: 4, z_lo: 2; z = z_hi * 2 + z_lo), core: 2. Of those that a mesh axis runs over, the one named last changes fastest.
Arguments:
- hidden: bfloat16 [4, 512, 5120], P('section', 'shard'), may hold values from -6 to 6
- w_qkv: bfloat16 [3, 5120, 5120], P(None, 'shard'), may hold values from -0.078125 to 0.078125
- q_gain: float32 [5120], replicated, may hold values from 0.5 to 2
- k_gain: float32 [5120], replicated, may hold values from 0.5 to 2
- modulation: float32 [4, 3, 5120], replicated, may hold values from -3 to 3
- step_index: int32 [4], P('section'), may hold values from 0 to 3
- cache_k: bfloat16 [7, 512, 5120], P(None, 'shard'), may hold values from -900 to 900
- cache_v: bfloat16 [7, 512, 5120], P(None, 'shard'), may hold values from -6 to 6
- slot_rank: int32 [7], replicated, may hold values from 0 to 6, each once
- visible: int32 [4], P('section'), may hold values from 1 to 7, as said below
Outputs:
- handed: bfloat16 [4, 512, 5120], P('section', 'shard')
The draws below stay inside these ranges and needn't reach their ends.
Inputs may be any that keep to these rules, and one draw needn't show every extreme that they name: slot_rank[c] counts the cached groups newer than the one in slot c. `visible`: some section has 7.
All inputs are finite; a program needn't handle non-finite values.
Results may differ from the reference program's by a relative error of at most 0.0055.
The reference program's roundings to bfloat16 on the way count: a program that leaves them out, or rounds other values in their place, can miss the bound.
Values may be sent and summed in bfloat16 or wider, within the bound.
No kernel may reach another device: no remote copies, remote signals or barrier semaphores. Data moves between devices by JAX's collectives and lax.ppermute only.
A program may use at most 128 MiB of HBM per device.

```python
import math
import jax
import jax.numpy as jnp
from jax import lax

D = 5120
HEADS = 40
HEAD = 128
TOK_DEV = 8
CACHE_CH = 7
TIMES = 4
SECTIONS = 4
GROUP = 512
N_SHARD = 64


def draw_cache_k(key, part):
    key = jax.random.fold_in(key, 11)
    key_base = jax.random.fold_in(key, 0)
    drawn = jax.random.normal(key_base, (CACHE_CH, GROUP, D), jnp.float32)
    return jnp.clip(drawn, -900.0, 900.0).astype(jnp.bfloat16)


def draw_visible(key, part):
    key = jax.random.fold_in(key, 5)
    key_count, key_full = jax.random.split(key, 2)
    counts = jax.random.randint(key_count, (SECTIONS,), 1, CACHE_CH + 1)
    full_section = jax.random.randint(key_full, (), 0, SECTIONS)
    return jnp.where(jnp.arange(SECTIONS) == full_section, CACHE_CH, counts).astype(jnp.int32)


def place_ends(values, key, least, high):
    longest = values.shape.index(max(values.shape))
    spots = []
    for shift in (0, 1):
        where = [jax.random.randint(jax.random.fold_in(key, axis), (), 0, length) for axis, length in enumerate(values.shape)]
        where[longest] = (where[longest] + shift) % values.shape[longest]
        spots.append(tuple(where))
    return values.at[spots[0]].set(least).at[spots[1]].set(high)


def block_scale(own_key, extent, pieces, low, top_value):
    def one(position, parts):
        steps = jax.random.uniform(jax.random.fold_in(jax.random.fold_in(own_key, 6), position), (parts,), jnp.float32, low / len(pieces), top_value / len(pieces))
        return jnp.repeat(jnp.exp(steps), extent[position] // parts).reshape((-1,) + (1,) * (len(extent) - position - 1))

    factor_of = one(*pieces[0])
    for cut in pieces[1:]:
        factor_of = factor_of * one(*cut)
    return factor_of


def bell_draw(own_key, extent, spread, limit, shards=(), dtype=jnp.bfloat16):
    values = spread * jax.random.normal(own_key, extent, jnp.float32)
    if shards:
        values = values * block_scale(own_key, extent, shards, -0.22, 0.18)
    return jnp.clip(values, -limit, limit).astype(dtype)


def setup_inputs(seed: int = 0) -> dict:
    key_list = jax.random.split(jax.random.key(seed), 11)
    return {
        "hidden": bell_draw(key_list[0], (SECTIONS, GROUP, D), 1.0, 6.0, ((0, 4), (1, 64))),
        "w_qkv": bell_draw(key_list[1], (3, D, D), D ** -0.5, 0.078125, ((1, 64),)),
        "q_gain": jnp.clip(jnp.exp(jax.random.uniform(key_list[2], (D,), jnp.float32, math.log(0.5), math.log(2.0))), 0.5, 2.0),
        "k_gain": jnp.clip(jnp.exp(jax.random.uniform(key_list[3], (D,), jnp.float32, math.log(0.5), math.log(2.0))), 0.5, 2.0),
        "modulation": bell_draw(key_list[4], (TIMES, 3, D), 0.5, 3.0, (), jnp.float32),
        "step_index": place_ends(jax.random.randint(key_list[5], (SECTIONS,), 0, TIMES), jax.random.fold_in(key_list[5], 1), 0, TIMES - 1).astype(jnp.int32),
        "cache_k": draw_cache_k(jax.random.fold_in(key_list[10], 71), 0),
        "cache_v": bell_draw(key_list[7], (CACHE_CH, GROUP, D), 1.0, 6.0, ((1, 64),)),
        "slot_rank": jax.random.permutation(key_list[8], CACHE_CH).astype(jnp.int32),
        "visible": draw_visible(jax.random.fold_in(key_list[10], 71), 0),
    }


epsilon = 1e-06

def project_rows(modulated, weight):
    return lax.dot_general(modulated, weight, (((1,), (1,)), ((), ())), preferred_element_type=jnp.float32)

def section_project(hidden_rows, mod_rows, w_qkv, q_gain, k_gain):
    tokens_f = hidden_rows.astype(jnp.float32)
    centered = tokens_f - lax.optimization_barrier(jnp.mean(tokens_f, axis=-1, keepdims=True))
    variance = lax.optimization_barrier(jnp.mean(centered * centered, axis=-1, keepdims=True))
    modulated = (centered * lax.rsqrt(variance + epsilon) * (1.0 + mod_rows[1]) + mod_rows[0]).astype(jnp.bfloat16)
    proj_q = project_rows(modulated, w_qkv[0])
    proj_k = project_rows(modulated, w_qkv[1])
    proj_v = project_rows(modulated, w_qkv[2])
    queries = (proj_q * lax.rsqrt(lax.optimization_barrier(jnp.mean(proj_q * proj_q, axis=-1, keepdims=True)) + epsilon) * q_gain).astype(jnp.bfloat16)
    keys = (proj_k * lax.rsqrt(lax.optimization_barrier(jnp.mean(proj_k * proj_k, axis=-1, keepdims=True)) + epsilon) * k_gain).astype(jnp.bfloat16)
    return (queries, keys, proj_v.astype(jnp.bfloat16))

def make_blocks(own_rows, cache_rows):
    own_part = own_rows.reshape(N_SHARD, 1, TOK_DEV, D)
    cache_part = cache_rows.reshape(CACHE_CH, N_SHARD, TOK_DEV, D).transpose(1, 0, 2, 3)
    joined = jnp.concatenate([own_part, cache_part], axis=1)
    return joined.reshape(N_SHARD, (CACHE_CH + 1) * TOK_DEV, HEADS, HEAD)

def reference(hidden, w_qkv, q_gain, k_gain, modulation, step_index, cache_k, cache_v, slot_rank, visible):
    all_mods = modulation[step_index]

    def project_one(inputs):
        return section_project(inputs[0], inputs[1], w_qkv, q_gain, k_gain)
    queries, keys, values = lax.map(project_one, (hidden, all_mods))
    written = (slot_rank == CACHE_CH - 1)[:, None, None]
    new_rank = (slot_rank + 1) % CACHE_CH
    new_cache_k = jnp.where(written, keys[SECTIONS - 1][None], cache_k)
    new_cache_v = jnp.where(written, values[SECTIONS - 1][None], cache_v)
    scale_by = 1.0 / math.sqrt(HEAD)

    def attend(inputs):
        query_rows, key_rows, value_rows, hidden_rows, mod_rows, count = inputs
        key_blocks = make_blocks(key_rows, new_cache_k)
        value_blocks = make_blocks(value_rows, new_cache_v)
        slot_seen = jnp.concatenate([jnp.ones((1,), jnp.bool_), new_rank < count])
        key_mask = jnp.repeat(slot_seen, TOK_DEV)
        query_f = query_rows.astype(jnp.float32).reshape(GROUP, HEADS, HEAD)

        def absorb(running, block):
            row_top, numer, denom = running
            block_keys, block_values = block
            scores = jnp.einsum('qhd,khd->hqk', query_f, block_keys.astype(jnp.float32)) * scale_by
            scores = jnp.where(key_mask[None, None, :], scores, -jnp.inf)
            block_max = lax.optimization_barrier(jnp.max(scores, axis=-1))
            weights = jnp.exp(scores - block_max[..., None])
            block_den = lax.optimization_barrier(jnp.sum(weights, axis=-1))
            rounded = lax.optimization_barrier(weights.astype(jnp.bfloat16))
            block_num = jnp.einsum('hqk,khd->hqd', rounded.astype(jnp.float32), block_values.astype(jnp.float32))
            new_top = jnp.maximum(row_top, block_max)
            old_scale = jnp.exp(row_top - new_top)
            new_scale = jnp.exp(block_max - new_top)
            numer = numer * old_scale[..., None] + block_num * new_scale[..., None]
            denom = denom * old_scale + block_den * new_scale
            return ((new_top, numer, denom), None)
        start_top = jnp.full((HEADS, GROUP), -jnp.inf, jnp.float32)
        start_num = jnp.zeros((HEADS, GROUP, HEAD), jnp.float32)
        start_den = jnp.zeros((HEADS, GROUP), jnp.float32)
        final, unused = lax.scan(absorb, (start_top, start_num, start_den), (key_blocks, value_blocks))
        attended = (final[1] / final[2][..., None]).transpose(1, 0, 2).reshape(GROUP, D)
        return (hidden_rows.astype(jnp.float32) + mod_rows[2] * attended).astype(jnp.bfloat16)
    layer_out = lax.map(attend, (queries, keys, values, hidden, all_mods, visible))
    return jnp.roll(layer_out, 1, axis=0)
```

```python
import math

import jax
import jax.numpy as jnp
from jax import lax
from jax.experimental import pallas as pl
from jax.experimental.pallas import tpu as pltpu
from jax.sharding import Mesh
from jax.sharding import PartitionSpec as P

AXES = ("zl", "core", "y", "zh1", "zh0", "x")
SIZES = (2, 2, 4, 2, 2, 4)
SECTION = ("zl", "core")
SHARD = ("y", "zh1", "zh0", "x")
GROUPS = ("y", "zh1")
MEMBERS = ("zh0", "x")

F32 = jnp.float32
BF16 = jnp.bfloat16
EPS = 1e-6
WIDTH = 5120
HEAD = 128
TOK = 8
SLOTS = 7
COLS = 80
PART = 640
PART_HEADS = 5
HALF_TOK = 256
CACHED = 896
TILE = 1280
VMEM_BYTES = 48 * 1024 * 1024


def params(**more):
    return pltpu.CompilerParams(vmem_limit_bytes=VMEM_BYTES, **more)


def swapped(value, axis):
    return lax.ppermute(value, axis, [(0, 1), (1, 0)])


def around(value, axis, by):
    length = lax.axis_size(axis)
    return lax.ppermute(value, axis, [(i, (i + by) % length) for i in range(length)])


def in_order(index, mine, other, axis=0):
    first = index == 0
    return jnp.concatenate(
        [jnp.where(first, mine, other), jnp.where(first, other, mine)], axis=axis
    )


def modulate_kernel(step_ref, hidden_ref, mod_ref, out_ref):
    tokens = hidden_ref[...].astype(F32)
    centered = tokens - jnp.mean(tokens, axis=-1, keepdims=True)
    variance = jnp.mean(centered * centered, axis=-1, keepdims=True)
    shift = mod_ref[0, 0:1, :]
    scale = mod_ref[0, 1:2, :]
    out_ref[...] = (centered * lax.rsqrt(variance + EPS) * (1.0 + scale) + shift).astype(BF16)


def modulate(hidden, modulation, step_index):
    return pl.pallas_call(
        modulate_kernel,
        grid_spec=pltpu.PrefetchScalarGridSpec(
            num_scalar_prefetch=1,
            grid=(1,),
            in_specs=[
                pl.BlockSpec((TOK, WIDTH), lambda i, step: (0, 0)),
                pl.BlockSpec((1, 3, WIDTH), lambda i, step: (step[0], 0, 0)),
            ],
            out_specs=pl.BlockSpec((TOK, WIDTH), lambda i, step: (0, 0)),
        ),
        out_shape=jax.ShapeDtypeStruct((TOK, WIDTH), BF16),
        compiler_params=params(),
        name="modulate",
    )(step_index, hidden, modulation)


def project_kernel(place_ref, x_ref, own_ref, near_ref, far_ref, q_ref, kv_ref, sums_ref, acc):
    step = pl.program_id(0)
    half = place_ref[1]
    mine = pl.multiple_of(half * COLS, 16)
    theirs = pl.multiple_of((1 - half) * COLS, 16)
    x = x_ref[...]

    @pl.when(step == 0)
    def _():
        acc[...] = jnp.zeros_like(acc)

    def add(rows, at):
        for i in range(3):
            acc[i, pl.ds(at, COLS), :] += lax.dot_general(
                rows[i], x, (((1,), (1,)), ((), ())), preferred_element_type=F32
            )

    add(own_ref, mine)

    @pl.when(step < 2)
    def _():
        add(near_ref, theirs)

    @pl.when(step >= 2)
    def _():
        add(far_ref, theirs)

    @pl.when(step == 3)
    def _():
        q, k, v = acc[0], acc[1], acc[2]
        q_ref[...] = q
        lane = lax.broadcasted_iota(jnp.int32, (2 * COLS, 128), 1)
        row = lax.broadcasted_iota(jnp.int32, (64, 128), 0) % 4
        q_sum = jnp.sum(q * q, axis=0, keepdims=True)
        k_sum = jnp.sum(k * k, axis=0, keepdims=True)
        sums_ref[:, 0:HALF_TOK] = jnp.broadcast_to(q_sum, (64, HALF_TOK))
        packed = jnp.zeros((64, 128), F32)
        for t in range(2):
            kt = k[:, 128 * t : 128 * t + 128]
            vt = v[:, 128 * t : 128 * t + 128]
            kv_ref[2 * t] = jnp.where(lane < 64, kt, pltpu.roll(vt, 64, 1))
            kv_ref[2 * t + 1] = jnp.where(lane < 64, pltpu.roll(kt, 64, 1), vt)
            st = jnp.broadcast_to(k_sum[:, 128 * t : 128 * t + 128], (64, 128))
            packed = jnp.where(row == 2 * t, st, packed)
            packed = jnp.where(row == 2 * t + 1, pltpu.roll(st, 64, 1), packed)
        sums_ref[:, HALF_TOK : HALF_TOK + 128] = packed


def project(place, x, own, near, far):
    def tile(j, place):
        return 2 * ((j // 2 + place[0]) % 2) + j % 2

    return pl.pallas_call(
        project_kernel,
        grid_spec=pltpu.PrefetchScalarGridSpec(
            num_scalar_prefetch=1,
            grid=(4,),
            in_specs=[
                pl.BlockSpec((HALF_TOK, TILE), lambda j, p: (0, tile(j, p))),
                pl.BlockSpec((3, COLS, TILE), lambda j, p: (0, 0, tile(j, p))),
                pl.BlockSpec((3, COLS, TILE), lambda j, p: (0, 0, jnp.minimum(j, 1))),
                pl.BlockSpec((3, COLS, TILE), lambda j, p: (0, 0, jnp.maximum(j - 2, 0))),
            ],
            out_specs=[
                pl.BlockSpec((2 * COLS, HALF_TOK), lambda j, p: (0, 0)),
                pl.BlockSpec((4, 2 * COLS, 128), lambda j, p: (0, 0, 0)),
                pl.BlockSpec((64, HALF_TOK + 128), lambda j, p: (0, 0)),
            ],
            scratch_shapes=[pltpu.VMEM((3, 2 * COLS, HALF_TOK), F32)],
        ),
        out_shape=[
            jax.ShapeDtypeStruct((2 * COLS, HALF_TOK), F32),
            jax.ShapeDtypeStruct((4, 2 * COLS, 128), F32),
            jax.ShapeDtypeStruct((64, HALF_TOK + 128), F32),
        ],
        compiler_params=params(),
        name="project",
    )(place, x, own, near, far)


def half_sums(sums_ref):
    total = sums_ref[0:8, :]
    for i in range(1, 8):
        total = total + sums_ref[8 * i : 8 * i + 8, :]
    return [jnp.sum(total[4 * h : 4 * h + 4, :], axis=0, keepdims=True) for h in range(2)]


def own_kernel(kv_ref, sums_ref, gain_ref, out_ref):
    lane = lax.broadcasted_iota(jnp.int32, (PART, 128), 1)
    gain = gain_ref[...]
    for h, total in enumerate(half_sums(sums_ref)):
        rate = lax.rsqrt(total[:, HALF_TOK : HALF_TOK + 128] / WIDTH + EPS)
        pieces = [kv_ref[4 * h + c, COLS * e : COLS * e + COLS, :] for e in range(2) for c in range(4)]
        joined = jnp.concatenate(pieces, axis=0)
        joined = jnp.where(lane < 64, joined * rate * gain, joined)
        for n in range(PART_HEADS):
            turned = joined[HEAD * n : HEAD * n + HEAD, :].T.astype(BF16)
            out_ref[0, 64 * h : 64 * h + 64, HEAD * n : HEAD * n + HEAD] = turned[0:64]
            out_ref[1, 64 * h : 64 * h + 64, HEAD * n : HEAD * n + HEAD] = turned[64:128]


def own_rows(kv, sums, gain):
    return pl.pallas_call(
        own_kernel,
        out_shape=jax.ShapeDtypeStruct((2, 128, PART), BF16),
        compiler_params=params(),
        name="own_rows",
    )(kv, sums, gain)


def attend_kernel(
    place_ref, q0, q1, q2, q3, sums_ref, gain_ref, cached_k, cached_v, own, fresh, bias_ref,
    out_ref, query, stats,
):
    head = pl.program_id(0)

    @pl.when(head == 0)
    def _():
        low, high = half_sums(sums_ref)
        total = jnp.where(place_ref[1] == 0, low, high)[:, 0:HALF_TOK]
        rate = lax.rsqrt(total / WIDTH + EPS)
        for by, piece in enumerate((q0, q1, q2, q3)):
            source = lax.rem(place_ref[2] + 4 - by, 4)
            for e in range(2):
                at = pl.multiple_of(source * COLS + e * (PART // 2), 16)
                rows = piece[COLS * e : COLS * e + COLS, :] * rate * gain_ref[pl.ds(at, COLS), :]
                query[pl.ds(at, COLS), :] = rows.astype(BF16)
        stats[...] = jnp.zeros_like(stats)

    q = query[pl.ds(pl.multiple_of(head * HEAD, HEAD), HEAD), :]
    factor = 1.0 / math.sqrt(HEAD)
    keys = (cached_k[0], own[0], fresh[0])
    values = (cached_v[0], own[1], fresh[1])
    scores = [jnp.dot(k, q, preferred_element_type=F32) * factor for k in keys]
    scores[0] = scores[0] + bias_ref[...]
    top = jnp.max(scores[0], axis=0, keepdims=True)
    for s in scores[1:]:
        top = jnp.maximum(top, jnp.max(s, axis=0, keepdims=True))
    den = jnp.zeros((1, HALF_TOK), F32)
    num = jnp.zeros((HEAD, HALF_TOK), F32)
    for s, v in zip(scores, values):
        w = jnp.exp(s - top)
        den = den + jnp.sum(w, axis=0, keepdims=True)
        num = num + lax.dot_general(
            v, w.astype(BF16), (((0,), (0,)), ((), ())), preferred_element_type=F32
        )
    rows = (num / den).T.astype(BF16)
    at = pl.multiple_of(head * HEAD, HEAD)
    for y in range(4):
        for x in range(4):
            out_ref[x, 16 * y : 16 * y + 16, pl.ds(at, HEAD)] = rows[16 * (4 * y + x) : 16 * (4 * y + x) + 16]
    stats[pl.ds(head, 1), :] = top
    stats[pl.ds(head + 8, 1), :] = den

    @pl.when(head == PART_HEADS - 1)
    def _():
        full = stats[0:16, :]
        hi = full.astype(BF16).astype(F32)
        mid = (full - hi).astype(BF16).astype(F32)
        low = full - hi - mid
        stats[0:16, :] = hi
        stats[16:32, :] = mid
        stats[32:48, :] = low
        turned = stats[...].T.astype(BF16)
        for y in range(4):
            for x in range(4):
                out_ref[x, 16 * y : 16 * y + 16, PART : PART + 128] = turned[
                    16 * (4 * y + x) : 16 * (4 * y + x) + 16
                ]


def attend(place, queries, sums, gain, cached, own, fresh, bias):
    whole = lambda *shape: pl.BlockSpec(shape, lambda h, p: (0,) * len(shape))
    return pl.pallas_call(
        attend_kernel,
        grid_spec=pltpu.PrefetchScalarGridSpec(
            num_scalar_prefetch=1,
            grid=(PART_HEADS,),
            in_specs=[whole(2 * COLS, HALF_TOK)] * 4
            + [
                whole(64, HALF_TOK + 128),
                whole(PART, 1),
                pl.BlockSpec((1, CACHED, HEAD), lambda h, p: (0, 0, h)),
                pl.BlockSpec((1, CACHED, HEAD), lambda h, p: (1, 0, h)),
                pl.BlockSpec((2, 128, HEAD), lambda h, p: (0, 0, h)),
                pl.BlockSpec((2, 128, HEAD), lambda h, p: (0, 0, h)),
                whole(CACHED, 1),
            ],
            out_specs=whole(4, 64, PART + 128),
            scratch_shapes=[
                pltpu.VMEM((PART, HALF_TOK), BF16),
                pltpu.VMEM((128, HALF_TOK), F32),
            ],
        ),
        out_shape=jax.ShapeDtypeStruct((4, 64, PART + 128), BF16),
        compiler_params=params(),
        name="attend",
    )(place, *queries, sums, gain, cached, cached, own, fresh, bias)


def join_kernel(in_ref, out_ref):
    tops, dens = [], []
    for j in range(4):
        parts = in_ref[j, :, PART : PART + 128].astype(F32)
        full = parts[:, 0:16] + parts[:, 16:32] + parts[:, 32:48]
        tops.append(full[:, 0:8])
        dens.append(full[:, 8:16])
    top = jnp.maximum(jnp.maximum(tops[0], tops[1]), jnp.maximum(tops[2], tops[3]))
    shares = [jnp.exp(t - top) * d for t, d in zip(tops, dens)]
    total = shares[0] + shares[1] + shares[2] + shares[3]
    for n in range(PART_HEADS):
        cols = slice(HEAD * n, HEAD * n + HEAD)
        joined = jnp.zeros((64, HEAD), F32)
        for j in range(4):
            joined = joined + in_ref[j, :, cols].astype(F32) * shares[j][:, n : n + 1]
        joined = joined / total[:, n : n + 1]
        for g in range(8):
            out_ref[g, :, cols] = joined[TOK * g : TOK * g + TOK]


def join(shares):
    return pl.pallas_call(
        join_kernel,
        out_shape=jax.ShapeDtypeStruct((8, TOK, PART), F32),
        compiler_params=params(),
        name="join",
    )(shares)


def finish_kernel(step_ref, att_ref, hidden_ref, mod_ref, out_ref):
    for g in range(8):
        cols = slice(PART * g, PART * g + PART)
        out_ref[:, cols] = (
            hidden_ref[:, cols].astype(F32) + mod_ref[0, 2:3, cols] * att_ref[g]
        ).astype(BF16)


def finish(attended, hidden, modulation, step_index):
    return pl.pallas_call(
        finish_kernel,
        grid_spec=pltpu.PrefetchScalarGridSpec(
            num_scalar_prefetch=1,
            grid=(1,),
            in_specs=[
                pl.BlockSpec((8, TOK, PART), lambda i, step: (0, 0, 0)),
                pl.BlockSpec((TOK, WIDTH), lambda i, step: (0, 0)),
                pl.BlockSpec((1, 3, WIDTH), lambda i, step: (step[0], 0, 0)),
            ],
            out_specs=pl.BlockSpec((TOK, WIDTH), lambda i, step: (0, 0)),
        ),
        out_shape=jax.ShapeDtypeStruct((TOK, WIDTH), BF16),
        compiler_params=params(),
        name="finish",
    )(step_index, attended, hidden, modulation)


def shards(
    hidden, w_qkv, q_gain, k_gain, modulation, step_index, cache_k, cache_v, slot_rank, visible
):
    zl, core = lax.axis_index("zl"), lax.axis_index("core")
    half, x_here = lax.axis_index("zh0"), lax.axis_index("x")
    section = lax.axis_index(SECTION)
    group = lax.axis_index(GROUPS)
    place = jnp.stack([core, half, x_here]).astype(jnp.int32)

    near = swapped(lax.dynamic_slice_in_dim(w_qkv, core * (WIDTH // 2), WIDTH // 2, 2), "zh0")
    far = swapped(near, "core")

    modulated = modulate(hidden[0], modulation, step_index)
    pair = in_order(lax.axis_index("zh1"), modulated, swapped(modulated, "zh1"))
    tokens = lax.all_to_all(
        jnp.broadcast_to(pair[None], (16,) + pair.shape), ("y", "x"), 0, 0, tiled=True
    ).reshape(HALF_TOK, WIDTH)

    caches = jnp.stack([cache_k, cache_v])
    quarter = lax.dynamic_slice_in_dim(caches, section * 2, 2, 2)
    quarter = quarter.reshape(2, SLOTS * 2, 8, PART).transpose(2, 0, 1, 3)
    quarter = lax.all_to_all(quarter, GROUPS, 0, 0, tiled=True)
    cached = quarter.transpose(1, 0, 2, 3).reshape(2, 8 * SLOTS * 2, PART)
    for axis in ("zh0", "zl", "core"):
        cached = jnp.concatenate([cached, swapped(cached, axis)], axis=1)
    new_rank = (slot_rank + 1) % SLOTS
    seen = (slot_rank != SLOTS - 1) & (new_rank < visible[0])
    bias = jnp.where(seen, 0.0, -jnp.inf).astype(F32)
    bias = jnp.tile(jnp.repeat(bias, 2), CACHED // (2 * SLOTS))[:, None]

    q_cols = lax.dynamic_slice_in_dim(q_gain, group * PART, PART)[:, None]
    k_cols = lax.dynamic_slice_in_dim(k_gain, group * PART, PART)[:, None]

    q_part, kv_part, sums = project(place, tokens, w_qkv, near, far)
    sums = lax.all_to_all(sums, SHARD, 0, 0, tiled=True)
    kv_sent = jnp.broadcast_to(kv_part[None], (2,) + kv_part.shape).reshape(8, 2 * COLS, 128)
    kv_all = lax.all_to_all(kv_sent, MEMBERS, 0, 0, tiled=True)
    queries = [q_part] + [around(q_part, "x", by) for by in (1, 2, 3)]
    own = own_rows(kv_all, sums, k_cols)
    across = lax.ppermute(own, SECTION, [(3, 1)])
    fresh = jnp.where((zl == 0) & (core == 1), across, own)
    beside = lax.ppermute(fresh, SECTION, [(3, 2), (1, 0)])
    fresh = jnp.where(core == 0, beside, fresh)
    shares = attend(place, queries, sums, q_cols, cached, own, fresh, bias)
    shares = lax.all_to_all(shares, "x", 0, 0, tiled=True)
    attended = lax.all_to_all(join(shares), GROUPS, 0, 0, tiled=True)
    layer_out = finish(attended, hidden[0], modulation, step_index)
    return around(layer_out[None], SECTION, 1)


def solution(mesh):
    fine = Mesh(mesh.devices.reshape(SIZES), AXES)
    return jax.shard_map(
        shards,
        mesh=fine,
        in_specs=(
            P(SECTION, SHARD, None),
            P(None, SHARD, None),
            P(),
            P(),
            P(),
            P(SECTION),
            P(None, SHARD, None),
            P(None, SHARD, None),
            P(),
            P(SECTION),
        ),
        out_specs=P(SECTION, SHARD, None),
        check_vma=False,
    )
```

```python
import functools
import math

import jax
import jax.numpy as jnp
from jax import lax
from jax.experimental import pallas as pl
from jax.experimental.pallas import tpu as pltpu
from jax.sharding import Mesh
from jax.sharding import PartitionSpec as P

AXES = ("zl", "core", "y", "zh1", "zh0", "x")
SIZES = (2, 2, 4, 2, 2, 4)
SECTION = ("zl", "core")
SHARD = ("y", "zh1", "zh0", "x")
GROUPS = ("y", "zh1")
MEMBERS = ("zh0", "x")

F32 = jnp.float32
BF16 = jnp.bfloat16
EPS = 1e-6
WIDTH = 5120
HEAD = 128
TOK = 8
SLOTS = 7
COLS = 80
PART = 640
PART_HEADS = 5
HALF_TOK = 256
CACHED = 896
TILE = 1280


def params(mebibytes):
    return pltpu.CompilerParams(vmem_limit_bytes=mebibytes * 1024 * 1024)


def swapped(value, axis):
    return lax.ppermute(value, axis, [(0, 1), (1, 0)])


def around(value, axis, by):
    length = lax.axis_size(axis)
    return lax.ppermute(value, axis, [(i, (i + by) % length) for i in range(length)])


def in_order(index, mine, other, axis=0):
    first = index == 0
    return jnp.concatenate(
        [jnp.where(first, mine, other), jnp.where(first, other, mine)], axis=axis
    )


def modulate_kernel(numbers_ref, place_ref, mine_ref, other_ref, mod_ref, out_ref):
    shift = mod_ref[0, 0:1, :]
    scale = mod_ref[0, 1:2, :]

    def of(ref):
        tokens = ref[...].astype(F32)
        centered = tokens - jnp.mean(tokens, axis=-1, keepdims=True)
        variance = jnp.mean(centered * centered, axis=-1, keepdims=True)
        return centered * lax.rsqrt(variance + EPS) * (1.0 + scale) + shift

    mine, other = of(mine_ref), of(other_ref)
    first = place_ref[5] == 0
    rows = jnp.concatenate(
        [jnp.where(first, mine, other), jnp.where(first, other, mine)], axis=0
    ).astype(BF16)
    for i in range(16):
        out_ref[i] = rows


def modulate(numbers, place, mine, other, modulation):
    return pl.pallas_call(
        modulate_kernel,
        grid_spec=pltpu.PrefetchScalarGridSpec(
            num_scalar_prefetch=2,
            grid=(1,),
            in_specs=[
                pl.BlockSpec((TOK, WIDTH), lambda i, n, p: (0, 0)),
                pl.BlockSpec((TOK, WIDTH), lambda i, n, p: (0, 0)),
                pl.BlockSpec((1, 3, WIDTH), lambda i, n, p: (n[0], 0, 0)),
            ],
            out_specs=pl.BlockSpec((16, 2 * TOK, WIDTH), lambda i, n, p: (0, 0, 0)),
        ),
        out_shape=jax.ShapeDtypeStruct((16, 2 * TOK, WIDTH), BF16),
        compiler_params=params(16),
        name="modulate",
    )(numbers, place, mine, other, modulation)


def project_kernel(
    place_ref, x_ref, own_ref, t0_ref, t1_ref, t2_ref, t3_ref,
    q_ref, kv_ref, sums_ref, m1_hbm, m2_hbm, m3_hbm, acc, m_ref, sem,
):
    step = pl.program_id(0)
    half = place_ref[1]
    mine = pl.multiple_of(half * 3 * COLS, 16)
    theirs = pl.multiple_of((1 - half) * 3 * COLS, 16)
    x = x_ref[...]

    @pl.when(step == 0)
    def _():
        acc[...] = jnp.zeros_like(acc)

    def add(weight, at):
        acc[pl.ds(at, 3 * COLS), :] += lax.dot_general(
            weight.reshape(3 * COLS, TILE), x, (((1,), (1,)), ((), ())), preferred_element_type=F32
        )

    add(own_ref[...], mine)
    for i, theirs_ref in enumerate((t0_ref, t1_ref, t2_ref, t3_ref)):

        @pl.when(step == i)
        def _(theirs_ref=theirs_ref):
            add(theirs_ref[...], theirs)

    @pl.when(step == 3)
    def _():
        q, k, v = [
            jnp.concatenate(
                [acc[(3 * e + i) * COLS : (3 * e + i + 1) * COLS, :] for e in range(2)], axis=0
            )
            for i in range(3)
        ]
        q_ref[...] = q
        for i in range(3):
            m_ref[i, :, 0:HALF_TOK] = q
        lane = lax.broadcasted_iota(jnp.int32, (2 * COLS, 128), 1)
        quarters = []
        for t in range(2):
            kt = k[:, 128 * t : 128 * t + 128]
            vt = v[:, 128 * t : 128 * t + 128]
            quarters.append(jnp.where(lane < 64, kt, pltpu.roll(vt, 64, 1)))
            quarters.append(jnp.where(lane < 64, pltpu.roll(kt, 64, 1), vt))
        for here in range(4):

            @pl.when(place_ref[2] == here)
            def _(here=here):
                kv_ref[...] = quarters[here]
                for i in range(3):
                    m_ref[i, :, HALF_TOK : HALF_TOK + 128] = quarters[here ^ (i + 1)]

        copies = [
            pltpu.make_async_copy(m_ref.at[i], to, sem.at[i])
            for i, to in enumerate((m1_hbm, m2_hbm, m3_hbm))
        ]
        for copy in copies:
            copy.start()
        sub = lax.broadcasted_iota(jnp.int32, (TOK, 128), 0)
        tile = jnp.zeros((TOK, 128), F32)
        for i, part in enumerate((q, k)):
            total = jnp.sum(part * part, axis=0, keepdims=True)
            for t in range(2):
                tile = jnp.where(sub == 2 * i + t, total[:, 128 * t : 128 * t + 128], tile)
        for i in range(32):
            sums_ref[i] = tile
        for copy in copies:
            copy.wait()


def project(place, x, own, theirs):
    def tile(j, place):
        return 2 * ((j % 2 + place[3]) % 2) + (j // 2 + place[0]) % 2

    piece = pl.BlockSpec((3, COLS, TILE), lambda j, p: (0, 0, 0))
    whole = lambda *shape: pl.BlockSpec(shape, lambda j, p: (0,) * len(shape))
    both = (2 * COLS, HALF_TOK + 128)
    outs = [(2 * COLS, HALF_TOK), (2 * COLS, 128), (32, TOK, 128)]
    return pl.pallas_call(
        project_kernel,
        grid_spec=pltpu.PrefetchScalarGridSpec(
            num_scalar_prefetch=1,
            grid=(4,),
            in_specs=[
                pl.BlockSpec((HALF_TOK, TILE), lambda j, p: (0, tile(j, p))),
                pl.BlockSpec((3, COLS, TILE), lambda j, p: (0, 0, tile(j, p))),
                piece, piece, piece, piece,
            ],
            out_specs=[whole(*shape) for shape in outs] + [pl.BlockSpec(memory_space=pltpu.HBM)] * 3,
            scratch_shapes=[
                pltpu.VMEM((6 * COLS, HALF_TOK), F32),
                pltpu.VMEM((3,) + both, F32),
                pltpu.SemaphoreType.DMA((3,)),
            ],
        ),
        out_shape=[jax.ShapeDtypeStruct(shape, F32) for shape in outs + [both] * 3],
        compiler_params=params(24),
        name="project",
    )(place, x, own, *theirs)


def gather_rows(place_ref, mine, messages, columns, held, sem, rate, gain_ref, out_ref, lanes=None):
    copies = [
        pltpu.make_async_copy(m.at[:, columns], held.at[i], sem.at[i]) for i, m in enumerate(messages)
    ]
    for copy in copies:
        copy.start()
    for i in range(4):
        if i:
            copies[i - 1].wait()
        for e in range(2):
            at = pl.multiple_of((place_ref[2] ^ i) * COLS + e * (PART // 2), 16)
            part = slice(COLS * e, COLS * e + COLS)
            raw = held[i - 1, part, :] if i else mine[part, :]
            rows = raw * rate * gain_ref[pl.ds(at, COLS), :]
            if lanes is not None:
                rows = jnp.where(lanes, rows, raw)
            out_ref[pl.ds(at, COLS), :] = rows.astype(BF16)


def all_rates(sums_ref):
    picked = [sums_ref[g] for g in range(32)]
    while len(picked) > 1:
        picked = [a + b for a, b in zip(picked[0::2], picked[1::2])]
    return lax.rsqrt(picked[0] / WIDTH + EPS)


def own_kernel(place_ref, kv0_ref, m1_hbm, m2_hbm, m3_hbm, sums_ref, gain_ref, out_ref, held, sem):
    rates = all_rates(sums_ref)
    rate = jnp.where(place_ref[2] < 2, rates[2:3, :], rates[3:4, :])
    rate = jnp.broadcast_to(rate, (TOK, 128))
    rate = jnp.where(place_ref[2] % 2 == 0, rate, pltpu.roll(rate, 64, 1))[0:1, :]
    lanes = lax.broadcasted_iota(jnp.int32, (COLS, 128), 1) < 64
    gather_rows(
        place_ref, kv0_ref, (m1_hbm, m2_hbm, m3_hbm), pl.ds(HALF_TOK, 128), held, sem,
        rate, gain_ref, out_ref, lanes,
    )


def own_rows(place, kv, messages, sums, gain):
    vmem = pl.BlockSpec(memory_space=pltpu.VMEM)
    return pl.pallas_call(
        own_kernel,
        in_specs=[pl.BlockSpec(memory_space=pltpu.SMEM), vmem]
        + [pl.BlockSpec(memory_space=pltpu.HBM)] * 3
        + [vmem, vmem],
        out_specs=vmem,
        scratch_shapes=[pltpu.VMEM((3, 2 * COLS, 128), F32), pltpu.SemaphoreType.DMA((3,))],
        out_shape=jax.ShapeDtypeStruct((PART, 128), BF16),
        compiler_params=params(8),
        name="own_rows",
    )(place, kv, *messages, sums, gain)


def absorb(q, parts, top, den, num):
    rate = math.log2(math.e) / math.sqrt(HEAD)
    turned = (((0,), (0,)), ((), ()))
    scores = []
    for part in parts:
        if isinstance(part, tuple):
            scores.append(jnp.dot(part[0], q, preferred_element_type=F32) + part[2])
        else:
            scores.append(lax.dot_general(part, q, turned, preferred_element_type=F32)[0:64])
    new_top = functools.reduce(
        jnp.maximum, [jnp.max(s, axis=0, keepdims=True) for s in scores] + ([] if top is None else [top])
    )
    if top is not None:
        factor = jnp.exp2((top - new_top) * rate)
        den, num = den * factor, num * factor
    else:
        den, num = jnp.zeros(new_top.shape, F32), jnp.zeros(q.shape, F32)
    for s, part in zip(scores, parts):
        w = jnp.exp2((s - new_top) * rate)
        den = den + jnp.sum(w, axis=0, keepdims=True)
        w = w.astype(BF16)
        if isinstance(part, tuple):
            num = num + lax.dot_general(part[1], w, turned, preferred_element_type=F32)
        else:
            w = jnp.concatenate([jnp.zeros_like(w), w], axis=0)
            num = num + jnp.dot(part, w, preferred_element_type=F32)
    return new_top, den, num


def attend_kernel(
    place_ref, q0, m1_hbm, m2_hbm, m3_hbm, sums_ref, gain_ref, c0, c1, c2, c3, own, bias_ref,
    query, stats, num_ref, held, sem,
):
    head = pl.program_id(0)

    @pl.when(head == 0)
    def _():
        rates = all_rates(sums_ref)
        rate = jnp.concatenate([rates[0:1, :], rates[1:2, :]], axis=1)
        gather_rows(
            place_ref, q0, (m1_hbm, m2_hbm, m3_hbm), pl.ds(0, HALF_TOK), held, sem,
            rate, gain_ref, query,
        )

    q = query[pl.ds(pl.multiple_of(head * HEAD, HEAD), HEAD), :]
    parts = [(c[0], c[1], bias_ref[...]) for c in (c0, c1, c2, c3)] + [own[...]]
    top, den, num = absorb(q, parts, None, None, None)
    num_ref[...] = num
    stats[0, 0:1, :] = top
    stats[0, 1:2, :] = den


def attend(place, query, messages, sums, gain, cached, own, bias):
    cached_spec = pl.BlockSpec((2, CACHED // 4, HEAD), lambda h, p: (0, 0, h))
    whole = lambda *shape: pl.BlockSpec(shape, lambda h, p: (0,) * len(shape))
    return pl.pallas_call(
        attend_kernel,
        grid_spec=pltpu.PrefetchScalarGridSpec(
            num_scalar_prefetch=1,
            grid=(PART_HEADS,),
            in_specs=[whole(2 * COLS, HALF_TOK)]
            + [pl.BlockSpec(memory_space=pltpu.HBM)] * 3
            + [whole(32, TOK, 128), whole(PART, 1)]
            + [cached_spec] * 4
            + [pl.BlockSpec((HEAD, 128), lambda h, p: (h, 0)), whole(CACHED // 4, 1)],
            out_specs=[
                whole(PART, HALF_TOK),
                pl.BlockSpec((1, 8, HALF_TOK), lambda h, p: (h, 0, 0)),
                pl.BlockSpec((HEAD, HALF_TOK), lambda h, p: (h, 0)),
            ],
            scratch_shapes=[pltpu.VMEM((3, 2 * COLS, HALF_TOK), F32), pltpu.SemaphoreType.DMA((3,))],
        ),
        out_shape=[
            jax.ShapeDtypeStruct((PART, HALF_TOK), BF16),
            jax.ShapeDtypeStruct((PART_HEADS, 8, HALF_TOK), F32),
            jax.ShapeDtypeStruct((PART, HALF_TOK), F32),
        ],
        compiler_params=params(14),
        cost_estimate=pl.CostEstimate(flops=700_000_000, bytes_accessed=5_000_000, transcendentals=1_300_000),
        name="attend",
    )(place, query, *messages, sums, gain, *cached, own, bias)


def close_kernel(place_ref, query, stats_ref, num_ref, near, spread, beside, out_ref, stats):
    stats[...] = jnp.zeros_like(stats)
    first = place_ref[0] == 0

    for h in range(PART_HEADS):
        cols = slice(HEAD * h, HEAD * h + HEAD)
        parts = [
            near[cols, :],
            jnp.where(first, spread[0, cols, :], beside[0, cols, :]),
            jnp.where(first, spread[1, cols, :], beside[1, cols, :]),
        ]
        top, den, num = absorb(
            query[cols, :], parts, stats_ref[h, 0:1, :], stats_ref[h, 1:2, :], num_ref[cols, :]
        )
        out_ref[:, cols] = (num / den).T.astype(BF16)
        stats[h : h + 1, :] = top
        stats[h + 8 : h + 9, :] = den
    full = stats[0:16, :]
    hi = full.astype(BF16).astype(F32)
    mid = (full - hi).astype(BF16).astype(F32)
    stats[0:16, :] = hi
    stats[16:32, :] = mid
    stats[32:48, :] = full - hi - mid
    out_ref[:, PART : PART + 128] = stats[...].T.astype(BF16)


def close(place, query, stats, num, fresh):
    vmem = pl.BlockSpec(memory_space=pltpu.VMEM)
    return pl.pallas_call(
        close_kernel,
        in_specs=[pl.BlockSpec(memory_space=pltpu.SMEM)] + [vmem] * 6,
        out_shape=jax.ShapeDtypeStruct((HALF_TOK, PART + 128), BF16),
        scratch_shapes=[pltpu.VMEM((128, HALF_TOK), F32)],
        compiler_params=params(8),
        name="close",
    )(place, query, stats, num, *fresh)


def finish_kernel(step_ref, in_ref, hidden_ref, mod_ref, out_ref):
    for g in range(8):
        tops, dens = [], []
        for j in range(4):
            parts = in_ref[8 * (g // 2) + 2 * j + g % 2, :, PART : PART + 128].astype(F32)
            full = parts[:, 0:16] + parts[:, 16:32] + parts[:, 32:48]
            tops.append(full[:, 0:8])
            dens.append(full[:, 8:16])
        top = jnp.maximum(jnp.maximum(tops[0], tops[1]), jnp.maximum(tops[2], tops[3]))
        shares = [jnp.exp((t - top) * (1.0 / math.sqrt(HEAD))) * d for t, d in zip(tops, dens)]
        total = shares[0] + shares[1] + shares[2] + shares[3]
        for n in range(PART_HEADS):
            cols = slice(HEAD * n, HEAD * n + HEAD)
            to = slice(PART * g + HEAD * n, PART * g + HEAD * n + HEAD)
            joined = jnp.zeros((TOK, HEAD), F32)
            for j in range(4):
                joined = joined + in_ref[8 * (g // 2) + 2 * j + g % 2, :, cols].astype(F32) * shares[j][:, n : n + 1]
            joined = joined / total[:, n : n + 1]
            out_ref[:, to] = (
                hidden_ref[:, to].astype(F32) + mod_ref[0, 2:3, to] * joined
            ).astype(BF16)


def finish(shares, hidden, modulation, step_index):
    return pl.pallas_call(
        finish_kernel,
        grid_spec=pltpu.PrefetchScalarGridSpec(
            num_scalar_prefetch=1,
            grid=(1,),
            in_specs=[
                pl.BlockSpec((32, TOK, PART + 128), lambda i, step: (0, 0, 0)),
                pl.BlockSpec((TOK, WIDTH), lambda i, step: (0, 0)),
                pl.BlockSpec((1, 3, WIDTH), lambda i, step: (step[0], 0, 0)),
            ],
            out_specs=pl.BlockSpec((TOK, WIDTH), lambda i, step: (0, 0)),
        ),
        out_shape=jax.ShapeDtypeStruct((TOK, WIDTH), BF16),
        compiler_params=params(8),
        name="finish",
    )(step_index, shares, hidden, modulation)


def flipped(value, axes, sizes, by):
    count = math.prod(sizes)
    return lax.ppermute(value, axes, [(i, i ^ by) for i in range(count)])


def shards(
    hidden, w_qkv, q_gain, k_gain, modulation, step_index, cache_k, cache_v, slot_rank, visible
):
    zl, core = lax.axis_index("zl"), lax.axis_index("core")
    zh1, half, x_here = lax.axis_index("zh1"), lax.axis_index("zh0"), lax.axis_index("x")
    y_here = lax.axis_index("y")
    fetch = lax.axis_index(SECTION)
    group = lax.axis_index(GROUPS)
    place = jnp.stack([core, half, x_here, zl, y_here, zh1]).astype(jnp.int32)

    moved = [(s, (s + 1) % 4) for s in range(4)]
    mine = lax.ppermute(hidden[0], SECTION, moved)
    other = lax.ppermute(
        hidden[0], SECTION + ("zh1",), [(2 * s + z, 2 * t + 1 - z) for s, t in moved for z in range(2)]
    )
    numbers = lax.ppermute(jnp.concatenate([step_index, visible]), SECTION, moved)

    w_sent = lax.dynamic_slice_in_dim(w_qkv, fetch * TILE, TILE, 2)
    w_sent, mine, other = lax.optimization_barrier((w_sent, mine, other))
    w0 = swapped(w_sent, "zh0")
    pair = modulate(numbers, place, mine, other, modulation)
    tokens = lax.all_to_all(pair, ("y", "x"), 0, 0, tiled=True).reshape(HALF_TOK, WIDTH)
    w0, cache_k, cache_v = lax.optimization_barrier((w0, cache_k, cache_v))
    w1 = swapped(w0, "zl")
    w2 = swapped(w0, "core")

    caches = jnp.stack([cache_k, cache_v]).reshape(2, SLOTS * TOK, WIDTH)
    towards = 2 * (y_here ^ fetch)
    c_same = lax.dynamic_slice_in_dim(caches, (towards + zh1) * PART, PART, 2)
    c_flip = lax.dynamic_slice_in_dim(caches, ((towards ^ 4) + 1 - zh1) * PART, PART, 2)
    places = [(f, y, z) for f in range(4) for y in range(4) for z in range(2)]
    spot = lambda f, y, z: 8 * f + 2 * y + z
    four = SECTION + GROUPS
    c_same = lax.ppermute(c_same, four, [(spot(f, y, z), spot(f, y ^ f, z)) for f, y, z in places])
    c_flip = lax.ppermute(
        c_flip, four, [(spot(f ^ 2, y, z), spot(f, y ^ f, 1 - z)) for f, y, z in places]
    )

    new_rank = (slot_rank + 1) % SLOTS
    seen = (slot_rank != SLOTS - 1) & (new_rank < numbers[1])
    bias = jnp.where(seen, 0.0, -jnp.inf).astype(F32)
    bias = jnp.tile(jnp.repeat(bias, TOK), CACHED // (4 * TOK * SLOTS))[:, None]
    q_cols = lax.dynamic_slice_in_dim(q_gain, group * PART, PART)[:, None]
    k_cols = lax.dynamic_slice_in_dim(k_gain, group * PART, PART)[:, None]

    w1, c_same, c_flip, bias, q_cols, k_cols = lax.optimization_barrier(
        (w1, c_same, c_flip, bias, q_cols, k_cols)
    )
    w3 = swapped(w1, "core")
    cached = jnp.concatenate([c_same, c_flip], axis=1)
    across = swapped(cached, "zh0")
    query, kv, sums, m1, m2, m3 = project(place, tokens, w_qkv, (w0, w1, w2, w3))
    messages = [flipped(m, "x", (4,), i) for i, m in ((1, m1), (2, m2), (3, m3))]
    sums = lax.all_to_all(sums, ("y", "zh1", "x"), 0, 0, tiled=True)
    messages, sums, across = lax.optimization_barrier((messages, sums, across))
    cached = jnp.concatenate([cached, across], axis=1)
    beyond = swapped(cached, "zl")
    beside = swapped(cached, "core")
    own = own_rows(place, kv, messages, sums, k_cols)
    near = swapped(own, "zh0")
    low = lax.ppermute(own, SECTION, [(0, 2)])
    high = lax.ppermute(own, SECTION + ("zh0",), [(h, 2 * 2 + 1 - h) for h in range(2)])
    near, low, high, beyond, beside = lax.optimization_barrier((near, low, high, beyond, beside))
    cached = [cached, beyond, beside, swapped(beyond, "core")]
    fresh = jnp.where(zl == 0, jnp.stack([own, near]), jnp.stack([low, high]))
    passed = lax.ppermute(fresh, SECTION, [(0, 1), (2, 3)])
    query, stats, num = attend(place, query, messages, sums, q_cols, cached, own, bias)
    shares = close(place, query, stats, num, [near, fresh, passed])
    shares = shares.reshape(32, TOK, PART + 128)
    shares = lax.all_to_all(shares, ("y", "x", "zh1"), 0, 0, tiled=True)
    return finish(shares, mine, modulation, numbers)[None]


def solution(mesh):
    fine = Mesh(mesh.devices.reshape(SIZES), AXES)
    return jax.shard_map(
        shards,
        mesh=fine,
        in_specs=(
            P(SECTION, SHARD, None),
            P(None, SHARD, None),
            P(),
            P(),
            P(),
            P(SECTION),
            P(None, SHARD, None),
            P(None, SHARD, None),
            P(),
            P(SECTION),
        ),
        out_specs=P(SECTION, SHARD, None),
        check_vma=False,
    )
```

```python
import functools
import math

import jax
import jax.numpy as jnp
from jax import lax
from jax.experimental import pallas as pl
from jax.experimental.pallas import tpu as pltpu
from jax.sharding import Mesh
from jax.sharding import PartitionSpec as P

AXES = ("zl", "core", "y", "zh1", "zh0", "x")
SIZES = (2, 2, 4, 2, 2, 4)
SECTION = ("zl", "core")
SHARD = ("y", "zh1", "zh0", "x")
GROUPS = ("y", "zh1")
MEMBERS = ("zh0", "x")

F32 = jnp.float32
BF16 = jnp.bfloat16
EPS = 1e-6
WIDTH = 5120
HEAD = 128
TOK = 8
SLOTS = 7
COLS = 80
PART = 640
PART_HEADS = 5
HALF_TOK = 256
CACHED = 896
TILE = 1280


def params(mebibytes):
    return pltpu.CompilerParams(vmem_limit_bytes=mebibytes * 1024 * 1024)


def swapped(value, axis):
    return lax.ppermute(value, axis, [(0, 1), (1, 0)])


def around(value, axis, by):
    length = lax.axis_size(axis)
    return lax.ppermute(value, axis, [(i, (i + by) % length) for i in range(length)])


def in_order(index, mine, other, axis=0):
    first = index == 0
    return jnp.concatenate(
        [jnp.where(first, mine, other), jnp.where(first, other, mine)], axis=axis
    )


def modulate_kernel(numbers_ref, place_ref, mine_ref, other_ref, mod_ref, out_ref):
    shift = mod_ref[0, 0:1, :]
    scale = mod_ref[0, 1:2, :]

    def of(ref):
        tokens = ref[...].astype(F32)
        centered = tokens - jnp.mean(tokens, axis=-1, keepdims=True)
        variance = jnp.mean(centered * centered, axis=-1, keepdims=True)
        return centered * lax.rsqrt(variance + EPS) * (1.0 + scale) + shift

    mine, other = of(mine_ref), of(other_ref)
    first = place_ref[5] == 0
    rows = jnp.concatenate(
        [jnp.where(first, mine, other), jnp.where(first, other, mine)], axis=0
    ).astype(BF16)
    out_ref[...] = rows


def modulate(numbers, place, mine, other, modulation):
    return pl.pallas_call(
        modulate_kernel,
        grid_spec=pltpu.PrefetchScalarGridSpec(
            num_scalar_prefetch=2,
            grid=(1,),
            in_specs=[
                pl.BlockSpec((TOK, WIDTH), lambda i, n, p: (0, 0)),
                pl.BlockSpec((TOK, WIDTH), lambda i, n, p: (0, 0)),
                pl.BlockSpec((1, 3, WIDTH), lambda i, n, p: (n[0], 0, 0)),
            ],
            out_specs=pl.BlockSpec((2 * TOK, WIDTH), lambda i, n, p: (0, 0)),
        ),
        out_shape=jax.ShapeDtypeStruct((2 * TOK, WIDTH), BF16),
        compiler_params=params(16),
        name="modulate",
    )(numbers, place, mine, other, modulation)


def project_kernel(
    place_ref, x0_hbm, x1_hbm, x2_hbm, x3_hbm, own_hbm, t0_hbm, t1_hbm, t2_hbm, t3_hbm,
    sums_hbm, m0_hbm, m1_hbm, m2_hbm, m3_hbm,
    x_ref, own_ref, t_ref, acc, m_ref, sums_ref, x_sem, own_sem, t_sem, out_sem,
):
    half = place_ref[1]
    mine = pl.multiple_of(half * 3 * COLS, 16)
    theirs = pl.multiple_of((1 - half) * 3 * COLS, 16)

    x_copies = []
    for j, x_hbm in enumerate((x0_hbm, x1_hbm, x2_hbm, x3_hbm)):
        for i in range(4):
            at = pl.multiple_of(64 * (place_ref[4] ^ j) + 16 * (place_ref[2] ^ i), 16)
            x_copies.append(
                pltpu.make_async_copy(
                    x_hbm.at[pl.ds(16 * i, 16), :], x_ref.at[pl.ds(at, 16), :], x_sem.at[4 * j + i]
                )
            )
    own_copies = [
        pltpu.make_async_copy(own_hbm.at[i], own_ref.at[pl.ds(COLS * i, COLS), :], own_sem.at[i])
        for i in range(3)
    ]
    t_copies = [
        pltpu.make_async_copy(t_hbm, t_ref.at[j], t_sem.at[j])
        for j, t_hbm in enumerate((t0_hbm, t1_hbm, t2_hbm, t3_hbm))
    ]
    for copy in x_copies + own_copies + t_copies:
        copy.start()

    def times(weight, x):
        return lax.dot_general(weight, x, (((1,), (1,)), ((), ())), preferred_element_type=F32)

    for copy in x_copies + own_copies:
        copy.wait()
    acc[pl.ds(mine, 3 * COLS), :] = times(own_ref[...], x_ref[...])
    for copy in t_copies:
        copy.wait()
    for tile in range(4):
        j = 2 * (place_ref[0] ^ (tile % 2)) + (place_ref[3] ^ (tile // 2))
        part = times(t_ref[j].reshape(3 * COLS, TILE), x_ref[:, TILE * tile : TILE * tile + TILE])
        if tile:
            acc[pl.ds(theirs, 3 * COLS), :] += part
        else:
            acc[pl.ds(theirs, 3 * COLS), :] = part

    q, k, v = [
        jnp.concatenate(
            [acc[(3 * e + i) * COLS : (3 * e + i + 1) * COLS, :] for e in range(2)], axis=0
        )
        for i in range(3)
    ]
    for i in range(4):
        m_ref[i, :, 0:HALF_TOK] = q
    lane = lax.broadcasted_iota(jnp.int32, (2 * COLS, 128), 1)
    quarters = []
    for t in range(2):
        kt = k[:, 128 * t : 128 * t + 128]
        vt = v[:, 128 * t : 128 * t + 128]
        quarters.append(jnp.where(lane < 64, kt, pltpu.roll(vt, 64, 1)))
        quarters.append(jnp.where(lane < 64, pltpu.roll(kt, 64, 1), vt))
    for here in range(4):

        @pl.when(place_ref[2] == here)
        def _(here=here):
            for i in range(4):
                m_ref[i, :, HALF_TOK : HALF_TOK + 128] = quarters[here ^ i]

    sub = lax.broadcasted_iota(jnp.int32, (TOK, 128), 0)
    tile = jnp.zeros((TOK, 128), F32)
    for i, part in enumerate((q, k)):
        total = jnp.sum(part * part, axis=0, keepdims=True)
        for t in range(2):
            tile = jnp.where(sub == 2 * i + t, total[:, 128 * t : 128 * t + 128], tile)
    for i in range(32):
        sums_ref[i] = tile
    copies = [
        pltpu.make_async_copy(m_ref.at[i], to, out_sem.at[i])
        for i, to in enumerate((m0_hbm, m1_hbm, m2_hbm, m3_hbm))
    ] + [pltpu.make_async_copy(sums_ref, sums_hbm, out_sem.at[4])]
    for copy in copies:
        copy.start()
    for copy in copies:
        copy.wait()


def project(place, x, own, theirs):
    both = (2 * COLS, HALF_TOK + 128)
    outs = [(32, TOK, 128), both, both, both, both]
    hbm = pl.BlockSpec(memory_space=pltpu.HBM)
    return pl.pallas_call(
        project_kernel,
        in_specs=[pl.BlockSpec(memory_space=pltpu.SMEM)] + [hbm] * 9,
        out_specs=[hbm] * 5,
        scratch_shapes=[
            pltpu.VMEM((HALF_TOK, WIDTH), BF16),
            pltpu.VMEM((3 * COLS, WIDTH), BF16),
            pltpu.VMEM((4, 3, COLS, TILE), BF16),
            pltpu.VMEM((6 * COLS, HALF_TOK), F32),
            pltpu.VMEM((4,) + both, F32),
            pltpu.VMEM((32, TOK, 128), F32),
            pltpu.SemaphoreType.DMA((16,)),
            pltpu.SemaphoreType.DMA((3,)),
            pltpu.SemaphoreType.DMA((4,)),
            pltpu.SemaphoreType.DMA((5,)),
        ],
        out_shape=[jax.ShapeDtypeStruct(shape, F32) for shape in outs],
        compiler_params=params(60),
        name="project",
    )(place, *x, own, *theirs)


def gather_rows(place_ref, pieces, held, sem, rate, gain_ref, out_ref, lanes=None):
    copies = [pltpu.make_async_copy(p, held.at[i], sem.at[i]) for i, p in enumerate(pieces)]
    for copy in copies:
        copy.start()
    for i, copy in enumerate(copies):
        copy.wait()
        for e in range(2):
            at = pl.multiple_of((place_ref[2] ^ i) * COLS + e * (PART // 2), 16)
            raw = held[i, COLS * e : COLS * e + COLS, :]
            rows = raw * rate * gain_ref[pl.ds(at, COLS), :]
            if lanes is not None:
                rows = jnp.where(lanes, rows, raw)
            out_ref[pl.ds(at, COLS), :] = rows.astype(BF16)


def all_rates(sums_ref):
    picked = [sums_ref[g] for g in range(32)]
    while len(picked) > 1:
        picked = [a + b for a, b in zip(picked[0::2], picked[1::2])]
    return lax.rsqrt(picked[0] / WIDTH + EPS)


def own_kernel(place_ref, m0_hbm, m1_hbm, m2_hbm, m3_hbm, sums_ref, gain_ref, out_ref, held, sem):
    rates = all_rates(sums_ref)
    rate = jnp.where(place_ref[2] < 2, rates[2:3, :], rates[3:4, :])
    rate = jnp.broadcast_to(rate, (TOK, 128))
    rate = jnp.where(place_ref[2] % 2 == 0, rate, pltpu.roll(rate, 64, 1))[0:1, :]
    lanes = lax.broadcasted_iota(jnp.int32, (COLS, 128), 1) < 64
    pieces = [m.at[:, pl.ds(HALF_TOK, 128)] for m in (m0_hbm, m1_hbm, m2_hbm, m3_hbm)]
    gather_rows(place_ref, pieces, held, sem, rate, gain_ref, out_ref, lanes)


def own_rows(place, messages, sums, gain):
    vmem = pl.BlockSpec(memory_space=pltpu.VMEM)
    return pl.pallas_call(
        own_kernel,
        in_specs=[pl.BlockSpec(memory_space=pltpu.SMEM)]
        + [pl.BlockSpec(memory_space=pltpu.HBM)] * 4
        + [vmem, vmem],
        out_specs=vmem,
        scratch_shapes=[pltpu.VMEM((4, 2 * COLS, 128), F32), pltpu.SemaphoreType.DMA((4,))],
        out_shape=jax.ShapeDtypeStruct((PART, 128), BF16),
        compiler_params=params(8),
        name="own_rows",
    )(place, *messages, sums, gain)


def absorb(q, parts, top, den, num):
    rate = math.log2(math.e) / math.sqrt(HEAD)
    turned = (((0,), (0,)), ((), ()))
    scores = []
    for part in parts:
        if isinstance(part, tuple):
            scores.append(jnp.dot(part[0], q, preferred_element_type=F32) + part[2])
        else:
            scores.append(lax.dot_general(part, q, turned, preferred_element_type=F32)[0:64])
    new_top = functools.reduce(
        jnp.maximum, [jnp.max(s, axis=0, keepdims=True) for s in scores] + ([] if top is None else [top])
    )
    if top is not None:
        factor = jnp.exp2((top - new_top) * rate)
        den, num = den * factor, num * factor
    else:
        den, num = jnp.zeros(new_top.shape, F32), jnp.zeros(q.shape, F32)
    for s, part in zip(scores, parts):
        w = jnp.exp2((s - new_top) * rate)
        den = den + jnp.sum(w, axis=0, keepdims=True)
        w = w.astype(BF16)
        if isinstance(part, tuple):
            num = num + lax.dot_general(part[1], w, turned, preferred_element_type=F32)
        else:
            w = jnp.concatenate([jnp.zeros_like(w), w], axis=0)
            num = num + jnp.dot(part, w, preferred_element_type=F32)
    return new_top, den, num


def attend_kernel(
    place_ref, m0_hbm, m1_hbm, m2_hbm, m3_hbm, sums_ref, gain_ref, c0, c1, c2, c3, own, bias_ref,
    query, stats, num_ref, held, sem,
):
    head = pl.program_id(0)

    @pl.when(head == 0)
    def _():
        rates = all_rates(sums_ref)
        rate = jnp.concatenate([rates[0:1, :], rates[1:2, :]], axis=1)
        pieces = [m.at[:, pl.ds(0, HALF_TOK)] for m in (m0_hbm, m1_hbm, m2_hbm, m3_hbm)]
        gather_rows(place_ref, pieces, held, sem, rate, gain_ref, query)

    q = query[pl.ds(pl.multiple_of(head * HEAD, HEAD), HEAD), :]
    parts = [(c[0], c[1], bias_ref[...]) for c in (c0, c1, c2, c3)] + [own[...]]
    top, den, num = absorb(q, parts, None, None, None)
    num_ref[...] = num
    stats[0, 0:1, :] = top
    stats[0, 1:2, :] = den


def attend(place, messages, sums, gain, cached, own, bias):
    cached_spec = pl.BlockSpec((2, CACHED // 4, HEAD), lambda h, p: (0, 0, h))
    whole = lambda *shape: pl.BlockSpec(shape, lambda h, p: (0,) * len(shape))
    return pl.pallas_call(
        attend_kernel,
        grid_spec=pltpu.PrefetchScalarGridSpec(
            num_scalar_prefetch=1,
            grid=(PART_HEADS,),
            in_specs=[pl.BlockSpec(memory_space=pltpu.HBM)] * 4
            + [whole(32, TOK, 128), whole(PART, 1)]
            + [cached_spec] * 4
            + [pl.BlockSpec((HEAD, 128), lambda h, p: (h, 0)), whole(CACHED // 4, 1)],
            out_specs=[
                whole(PART, HALF_TOK),
                pl.BlockSpec((1, 8, HALF_TOK), lambda h, p: (h, 0, 0)),
                pl.BlockSpec((HEAD, HALF_TOK), lambda h, p: (h, 0)),
            ],
            scratch_shapes=[pltpu.VMEM((4, 2 * COLS, HALF_TOK), F32), pltpu.SemaphoreType.DMA((4,))],
        ),
        out_shape=[
            jax.ShapeDtypeStruct((PART, HALF_TOK), BF16),
            jax.ShapeDtypeStruct((PART_HEADS, 8, HALF_TOK), F32),
            jax.ShapeDtypeStruct((PART, HALF_TOK), F32),
        ],
        compiler_params=params(14),
        cost_estimate=pl.CostEstimate(flops=700_000_000, bytes_accessed=5_000_000, transcendentals=1_300_000),
        name="attend",
    )(place, *messages, sums, gain, *cached, own, bias)


def close_kernel(place_ref, query, stats_ref, num_ref, near, spread, beside, out_ref, stats):
    stats[...] = jnp.zeros_like(stats)
    first = place_ref[0] == 0

    for h in range(PART_HEADS):
        cols = slice(HEAD * h, HEAD * h + HEAD)
        parts = [
            near[cols, :],
            jnp.where(first, spread[0, cols, :], beside[0, cols, :]),
            jnp.where(first, spread[1, cols, :], beside[1, cols, :]),
        ]
        top, den, num = absorb(
            query[cols, :], parts, stats_ref[h, 0:1, :], stats_ref[h, 1:2, :], num_ref[cols, :]
        )
        out_ref[:, cols] = (num / den).T.astype(BF16)
        stats[h : h + 1, :] = top
        stats[h + 8 : h + 9, :] = den
    full = stats[0:16, :]
    hi = full.astype(BF16).astype(F32)
    mid = (full - hi).astype(BF16).astype(F32)
    stats[0:16, :] = hi
    stats[16:32, :] = mid
    stats[32:48, :] = full - hi - mid
    out_ref[:, PART : PART + 128] = stats[...].T.astype(BF16)


def close(place, query, stats, num, fresh):
    vmem = pl.BlockSpec(memory_space=pltpu.VMEM)
    return pl.pallas_call(
        close_kernel,
        in_specs=[pl.BlockSpec(memory_space=pltpu.SMEM)] + [vmem] * 6,
        out_shape=jax.ShapeDtypeStruct((HALF_TOK, PART + 128), BF16),
        scratch_shapes=[pltpu.VMEM((128, HALF_TOK), F32)],
        compiler_params=params(8),
        name="close",
    )(place, query, stats, num, *fresh)


def finish_kernel(step_ref, in_ref, hidden_ref, mod_ref, out_ref):
    for g in range(8):
        tops, dens = [], []
        for j in range(4):
            parts = in_ref[8 * (g // 2) + 2 * j + g % 2, :, PART : PART + 128].astype(F32)
            full = parts[:, 0:16] + parts[:, 16:32] + parts[:, 32:48]
            tops.append(full[:, 0:8])
            dens.append(full[:, 8:16])
        top = jnp.maximum(jnp.maximum(tops[0], tops[1]), jnp.maximum(tops[2], tops[3]))
        shares = [jnp.exp((t - top) * (1.0 / math.sqrt(HEAD))) * d for t, d in zip(tops, dens)]
        total = shares[0] + shares[1] + shares[2] + shares[3]
        for n in range(PART_HEADS):
            cols = slice(HEAD * n, HEAD * n + HEAD)
            to = slice(PART * g + HEAD * n, PART * g + HEAD * n + HEAD)
            joined = jnp.zeros((TOK, HEAD), F32)
            for j in range(4):
                joined = joined + in_ref[8 * (g // 2) + 2 * j + g % 2, :, cols].astype(F32) * shares[j][:, n : n + 1]
            joined = joined / total[:, n : n + 1]
            out_ref[:, to] = (
                hidden_ref[:, to].astype(F32) + mod_ref[0, 2:3, to] * joined
            ).astype(BF16)


def finish(shares, hidden, modulation, step_index):
    return pl.pallas_call(
        finish_kernel,
        grid_spec=pltpu.PrefetchScalarGridSpec(
            num_scalar_prefetch=1,
            grid=(1,),
            in_specs=[
                pl.BlockSpec((32, TOK, PART + 128), lambda i, step: (0, 0, 0)),
                pl.BlockSpec((TOK, WIDTH), lambda i, step: (0, 0)),
                pl.BlockSpec((1, 3, WIDTH), lambda i, step: (step[0], 0, 0)),
            ],
            out_specs=pl.BlockSpec((TOK, WIDTH), lambda i, step: (0, 0)),
        ),
        out_shape=jax.ShapeDtypeStruct((TOK, WIDTH), BF16),
        compiler_params=params(8),
        name="finish",
    )(step_index, shares, hidden, modulation)


def flipped(value, axes, sizes, by):
    count = math.prod(sizes)
    return lax.ppermute(value, axes, [(i, i ^ by) for i in range(count)])


def shards(
    hidden, w_qkv, q_gain, k_gain, modulation, step_index, cache_k, cache_v, slot_rank, visible
):
    zl, core = lax.axis_index("zl"), lax.axis_index("core")
    zh1, half, x_here = lax.axis_index("zh1"), lax.axis_index("zh0"), lax.axis_index("x")
    y_here = lax.axis_index("y")
    fetch = lax.axis_index(SECTION)
    group = lax.axis_index(GROUPS)
    place = jnp.stack([core, half, x_here, zl, y_here, zh1]).astype(jnp.int32)

    moved = [(s, (s + 1) % 4) for s in range(4)]
    mine = lax.ppermute(hidden[0], SECTION, moved)
    other = lax.ppermute(
        hidden[0], SECTION + ("zh1",), [(2 * s + z, 2 * t + 1 - z) for s, t in moved for z in range(2)]
    )
    numbers = lax.ppermute(jnp.concatenate([step_index, visible]), SECTION, moved)

    w_sent = lax.dynamic_slice_in_dim(w_qkv, fetch * TILE, TILE, 2)
    w_sent, mine, other = lax.optimization_barrier((w_sent, mine, other))
    w0 = swapped(w_sent, "zh0")
    pair = modulate(numbers, place, mine, other, modulation)
    row = jnp.concatenate([pair] + [flipped(pair, "x", (4,), i) for i in (1, 2, 3)], axis=0)
    tokens = [flipped(row, "y", (4,), i) for i in (1, 2, 3)]
    w0, cache_k, cache_v, row = lax.optimization_barrier((w0, cache_k, cache_v, row))
    w1 = swapped(w0, "zl")
    w2 = swapped(w0, "core")

    caches = jnp.stack([cache_k, cache_v]).reshape(2, SLOTS * TOK, WIDTH)
    towards = 2 * (y_here ^ fetch)
    c_same = lax.dynamic_slice_in_dim(caches, (towards + zh1) * PART, PART, 2)
    c_flip = lax.dynamic_slice_in_dim(caches, ((towards ^ 4) + 1 - zh1) * PART, PART, 2)
    places = [(f, y, z) for f in range(4) for y in range(4) for z in range(2)]
    spot = lambda f, y, z: 8 * f + 2 * y + z
    four = SECTION + GROUPS
    c_same = lax.ppermute(c_same, four, [(spot(f, y, z), spot(f, y ^ f, z)) for f, y, z in places])
    c_flip = lax.ppermute(
        c_flip, four, [(spot(f ^ 2, y, z), spot(f, y ^ f, 1 - z)) for f, y, z in places]
    )

    new_rank = (slot_rank + 1) % SLOTS
    seen = (slot_rank != SLOTS - 1) & (new_rank < numbers[1])
    bias = jnp.where(seen, 0.0, -jnp.inf).astype(F32)
    bias = jnp.tile(jnp.repeat(bias, TOK), CACHED // (4 * TOK * SLOTS))[:, None]
    q_cols = lax.dynamic_slice_in_dim(q_gain, group * PART, PART)[:, None]
    k_cols = lax.dynamic_slice_in_dim(k_gain, group * PART, PART)[:, None]

    w1, tokens, c_same, c_flip, bias, q_cols, k_cols = lax.optimization_barrier(
        (w1, tokens, c_same, c_flip, bias, q_cols, k_cols)
    )
    w3 = swapped(w1, "core")
    cached = jnp.concatenate([c_same, c_flip], axis=1)
    across = swapped(cached, "zh0")
    tokens = [row] + tokens

    sums, m0, m1, m2, m3 = project(place, tokens, w_qkv, (w0, w1, w2, w3))
    messages = [m0] + [flipped(m, "x", (4,), i) for i, m in ((1, m1), (2, m2), (3, m3))]
    sums, across = lax.optimization_barrier((sums, across))
    cached = jnp.concatenate([cached, across], axis=1)
    sums = lax.all_to_all(sums, ("y", "zh1", "x"), 0, 0, tiled=True)
    beyond = swapped(cached, "zl")
    beside = swapped(cached, "core")
    messages, sums, beyond, beside = lax.optimization_barrier((messages, sums, beyond, beside))
    own = own_rows(place, messages, sums, k_cols)
    near = swapped(own, "zh0")
    low = lax.ppermute(own, SECTION, [(0, 2)])
    high = lax.ppermute(own, SECTION + ("zh0",), [(h, 2 * 2 + 1 - h) for h in range(2)])
    cached = [cached, beyond, beside, swapped(beyond, "core")]
    query, stats, num = attend(place, messages, sums, q_cols, cached, own, bias)
    near, low, high, num = lax.optimization_barrier((near, low, high, num))
    fresh = jnp.where(zl == 0, jnp.stack([own, near]), jnp.stack([low, high]))
    passed = lax.ppermute(fresh, SECTION, [(0, 1), (2, 3)])
    shares = close(place, query, stats, num, [near, fresh, passed])
    shares = shares.reshape(32, TOK, PART + 128)
    shares = lax.all_to_all(shares, ("y", "x", "zh1"), 0, 0, tiled=True)
    return finish(shares, mine, modulation, numbers)[None]


def solution(mesh):
    fine = Mesh(mesh.devices.reshape(SIZES), AXES)
    return jax.shard_map(
        shards,
        mesh=fine,
        in_specs=(
            P(SECTION, SHARD, None),
            P(None, SHARD, None),
            P(),
            P(),
            P(),
            P(SECTION),
            P(None, SHARD, None),
            P(None, SHARD, None),
            P(),
            P(SECTION),
        ),
        out_specs=P(SECTION, SHARD, None),
        check_vma=False,
    )
```

```python
import functools
import math

import jax
import jax.numpy as jnp
from jax import lax
from jax.experimental import pallas as pl
from jax.experimental.pallas import tpu as pltpu
from jax.sharding import Mesh
from jax.sharding import PartitionSpec as P

AXES = ("zl", "core", "y", "zh1", "zh0", "x")
SIZES = (2, 2, 4, 2, 2, 4)
SECTION = ("zl", "core")
SHARD = ("y", "zh1", "zh0", "x")
GROUPS = ("y", "zh1")
MEMBERS = ("zh0", "x")

F32 = jnp.float32
BF16 = jnp.bfloat16
EPS = 1e-6
WIDTH = 5120
HEAD = 128
TOK = 8
SLOTS = 7
COLS = 80
PART = 640
PART_HEADS = 5
HALF_TOK = 256
CACHED = 896
TILE = 1280


def params(mebibytes):
    return pltpu.CompilerParams(vmem_limit_bytes=mebibytes * 1024 * 1024)


def swapped(value, axis):
    return lax.ppermute(value, axis, [(0, 1), (1, 0)])


def around(value, axis, by):
    length = lax.axis_size(axis)
    return lax.ppermute(value, axis, [(i, (i + by) % length) for i in range(length)])


def in_order(index, mine, other, axis=0):
    first = index == 0
    return jnp.concatenate(
        [jnp.where(first, mine, other), jnp.where(first, other, mine)], axis=axis
    )


def modulate_kernel(numbers_ref, place_ref, mine_ref, other_ref, mod_ref, out_ref):
    shift = mod_ref[0, 0:1, :]
    scale = mod_ref[0, 1:2, :]

    def of(ref):
        tokens = ref[...].astype(F32)
        centered = tokens - jnp.mean(tokens, axis=-1, keepdims=True)
        variance = jnp.mean(centered * centered, axis=-1, keepdims=True)
        return centered * lax.rsqrt(variance + EPS) * (1.0 + scale) + shift

    mine, other = of(mine_ref), of(other_ref)
    first = place_ref[5] == 0
    rows = jnp.concatenate(
        [jnp.where(first, mine, other), jnp.where(first, other, mine)], axis=0
    ).astype(BF16)
    out_ref[...] = rows


def modulate(numbers, place, mine, other, modulation):
    return pl.pallas_call(
        modulate_kernel,
        grid_spec=pltpu.PrefetchScalarGridSpec(
            num_scalar_prefetch=2,
            grid=(1,),
            in_specs=[
                pl.BlockSpec((TOK, WIDTH), lambda i, n, p: (0, 0)),
                pl.BlockSpec((TOK, WIDTH), lambda i, n, p: (0, 0)),
                pl.BlockSpec((1, 3, WIDTH), lambda i, n, p: (n[0], 0, 0)),
            ],
            out_specs=pl.BlockSpec((2 * TOK, WIDTH), lambda i, n, p: (0, 0)),
        ),
        out_shape=jax.ShapeDtypeStruct((2 * TOK, WIDTH), BF16),
        compiler_params=params(16),
        name="modulate",
    )(numbers, place, mine, other, modulation)


def project_kernel(
    place_ref, x0_hbm, x1_hbm, x2_hbm, x3_hbm, own_hbm, t0_hbm, t1_hbm, t2_hbm, t3_hbm,
    sums_hbm, m0_hbm, m1_hbm, m2_hbm, m3_hbm,
    x_ref, own_ref, t_ref, acc, m_ref, sums_ref, x_sem, own_sem, t_sem, out_sem,
):
    half = place_ref[1]
    mine = pl.multiple_of(half * 3 * COLS, 16)
    theirs = pl.multiple_of((1 - half) * 3 * COLS, 16)

    x_copies = []
    for j, x_hbm in enumerate((x0_hbm, x1_hbm, x2_hbm, x3_hbm)):
        for i in range(4):
            at = pl.multiple_of(64 * (place_ref[4] ^ j) + 16 * (place_ref[2] ^ i), 16)
            x_copies.append(
                pltpu.make_async_copy(
                    x_hbm.at[pl.ds(16 * i, 16), :], x_ref.at[pl.ds(at, 16), :], x_sem.at[4 * j + i]
                )
            )
    own_copies = [
        pltpu.make_async_copy(own_hbm.at[i], own_ref.at[pl.ds(COLS * i, COLS), :], own_sem.at[i])
        for i in range(3)
    ]
    t_copies = [
        pltpu.make_async_copy(t_hbm, t_ref.at[j], t_sem.at[j])
        for j, t_hbm in enumerate((t0_hbm, t1_hbm, t2_hbm, t3_hbm))
    ]
    for copy in x_copies + own_copies + t_copies:
        copy.start()

    def times(weight, x):
        return lax.dot_general(weight, x, (((1,), (1,)), ((), ())), preferred_element_type=F32)

    for copy in x_copies + own_copies:
        copy.wait()
    acc[pl.ds(mine, 3 * COLS), :] = times(own_ref[...], x_ref[...])
    for copy in t_copies:
        copy.wait()
    for tile in range(4):
        j = 2 * (place_ref[0] ^ (tile % 2)) + (place_ref[3] ^ (tile // 2))
        part = times(t_ref[j].reshape(3 * COLS, TILE), x_ref[:, TILE * tile : TILE * tile + TILE])
        if tile:
            acc[pl.ds(theirs, 3 * COLS), :] += part
        else:
            acc[pl.ds(theirs, 3 * COLS), :] = part

    q, k, v = [
        jnp.concatenate(
            [acc[(3 * e + i) * COLS : (3 * e + i + 1) * COLS, :] for e in range(2)], axis=0
        )
        for i in range(3)
    ]
    for i in range(4):
        m_ref[i, :, 0:HALF_TOK] = q
    lane = lax.broadcasted_iota(jnp.int32, (2 * COLS, 128), 1)
    quarters = []
    for t in range(2):
        kt = k[:, 128 * t : 128 * t + 128]
        vt = v[:, 128 * t : 128 * t + 128]
        quarters.append(jnp.where(lane < 64, kt, pltpu.roll(vt, 64, 1)))
        quarters.append(jnp.where(lane < 64, pltpu.roll(kt, 64, 1), vt))
    for here in range(4):

        @pl.when(place_ref[2] == here)
        def _(here=here):
            for i in range(4):
                m_ref[i, :, HALF_TOK : HALF_TOK + 128] = quarters[here ^ i]

    sub = lax.broadcasted_iota(jnp.int32, (TOK, 128), 0)
    tile = jnp.zeros((TOK, 128), F32)
    for i, part in enumerate((q, k)):
        total = jnp.sum(part * part, axis=0, keepdims=True)
        for t in range(2):
            tile = jnp.where(sub == 2 * i + t, total[:, 128 * t : 128 * t + 128], tile)
    for i in range(32):
        sums_ref[i] = tile
    copies = [
        pltpu.make_async_copy(m_ref.at[i], to, out_sem.at[i])
        for i, to in enumerate((m0_hbm, m1_hbm, m2_hbm, m3_hbm))
    ] + [pltpu.make_async_copy(sums_ref, sums_hbm, out_sem.at[4])]
    for copy in copies:
        copy.start()
    for copy in copies:
        copy.wait()


def project(place, x, own, theirs):
    both = (2 * COLS, HALF_TOK + 128)
    outs = [(32, TOK, 128), both, both, both, both]
    hbm = pl.BlockSpec(memory_space=pltpu.HBM)
    return pl.pallas_call(
        project_kernel,
        in_specs=[pl.BlockSpec(memory_space=pltpu.SMEM)] + [hbm] * 9,
        out_specs=[hbm] * 5,
        scratch_shapes=[
            pltpu.VMEM((HALF_TOK, WIDTH), BF16),
            pltpu.VMEM((3 * COLS, WIDTH), BF16),
            pltpu.VMEM((4, 3, COLS, TILE), BF16),
            pltpu.VMEM((6 * COLS, HALF_TOK), F32),
            pltpu.VMEM((4,) + both, F32),
            pltpu.VMEM((32, TOK, 128), F32),
            pltpu.SemaphoreType.DMA((16,)),
            pltpu.SemaphoreType.DMA((3,)),
            pltpu.SemaphoreType.DMA((4,)),
            pltpu.SemaphoreType.DMA((5,)),
        ],
        out_shape=[jax.ShapeDtypeStruct(shape, F32) for shape in outs],
        compiler_params=params(60),
        name="project",
    )(place, *x, own, *theirs)


def gather_rows(place_ref, pieces, held, sem, rate, gain_ref, out_ref, lanes=None):
    copies = [pltpu.make_async_copy(p, held.at[i], sem.at[i]) for i, p in enumerate(pieces)]
    for copy in copies:
        copy.start()
    for i, copy in enumerate(copies):
        copy.wait()
        for e in range(2):
            at = pl.multiple_of((place_ref[2] ^ i) * COLS + e * (PART // 2), 16)
            raw = held[i, COLS * e : COLS * e + COLS, :]
            rows = raw * rate * gain_ref[pl.ds(at, COLS), :]
            if lanes is not None:
                rows = jnp.where(lanes, rows, raw)
            out_ref[pl.ds(at, COLS), :] = rows.astype(BF16)


def all_rates(sums_ref):
    picked = [sums_ref[g] for g in range(32)]
    while len(picked) > 1:
        picked = [a + b for a, b in zip(picked[0::2], picked[1::2])]
    return lax.rsqrt(picked[0] / WIDTH + EPS)


def own_kernel(place_ref, m0_hbm, m1_hbm, m2_hbm, m3_hbm, sums_ref, gain_ref, out_ref, held, sem):
    rates = all_rates(sums_ref)
    rate = jnp.where(place_ref[2] < 2, rates[2:3, :], rates[3:4, :])
    rate = jnp.broadcast_to(rate, (TOK, 128))
    rate = jnp.where(place_ref[2] % 2 == 0, rate, pltpu.roll(rate, 64, 1))[0:1, :]
    lanes = lax.broadcasted_iota(jnp.int32, (COLS, 128), 1) < 64
    pieces = [m.at[:, pl.ds(HALF_TOK, 128)] for m in (m0_hbm, m1_hbm, m2_hbm, m3_hbm)]
    gather_rows(place_ref, pieces, held, sem, rate, gain_ref, out_ref, lanes)


def own_rows(place, messages, sums, gain):
    vmem = pl.BlockSpec(memory_space=pltpu.VMEM)
    return pl.pallas_call(
        own_kernel,
        in_specs=[pl.BlockSpec(memory_space=pltpu.SMEM)]
        + [pl.BlockSpec(memory_space=pltpu.HBM)] * 4
        + [vmem, vmem],
        out_specs=vmem,
        scratch_shapes=[pltpu.VMEM((4, 2 * COLS, 128), F32), pltpu.SemaphoreType.DMA((4,))],
        out_shape=jax.ShapeDtypeStruct((PART, 128), BF16),
        compiler_params=params(8),
        name="own_rows",
    )(place, *messages, sums, gain)


def absorb(q, parts, top, den, num):
    rate = math.log2(math.e) / math.sqrt(HEAD)
    turned = (((0,), (0,)), ((), ()))
    scores = []
    for part in parts:
        if isinstance(part, tuple):
            scores.append(jnp.dot(part[0], q, preferred_element_type=F32) + part[2])
        else:
            scores.append(lax.dot_general(part, q, turned, preferred_element_type=F32)[0:64])
    new_top = functools.reduce(
        jnp.maximum, [jnp.max(s, axis=0, keepdims=True) for s in scores] + ([] if top is None else [top])
    )
    if top is not None:
        factor = jnp.exp2((top - new_top) * rate)
        den, num = den * factor, num * factor
    else:
        den, num = jnp.zeros(new_top.shape, F32), jnp.zeros(q.shape, F32)
    for s, part in zip(scores, parts):
        w = jnp.exp2((s - new_top) * rate)
        den = den + jnp.sum(w, axis=0, keepdims=True)
        w = w.astype(BF16)
        if isinstance(part, tuple):
            num = num + lax.dot_general(part[1], w, turned, preferred_element_type=F32)
        else:
            w = jnp.concatenate([jnp.zeros_like(w), w], axis=0)
            num = num + jnp.dot(part, w, preferred_element_type=F32)
    return new_top, den, num


def attend_kernel(
    place_ref, m0_hbm, m1_hbm, m2_hbm, m3_hbm, sums_ref, gain_ref, c0, c1, c2, c3, own, bias_ref,
    query, stats, num_ref, held, sem,
):
    rates = all_rates(sums_ref)
    rate = jnp.concatenate([rates[0:1, :], rates[1:2, :]], axis=1)
    pieces = [m.at[:, pl.ds(0, HALF_TOK)] for m in (m0_hbm, m1_hbm, m2_hbm, m3_hbm)]
    gather_rows(place_ref, pieces, held, sem, rate, gain_ref, query)
    bias = bias_ref[...]
    for head in range(PART_HEADS):
        cols = slice(HEAD * head, HEAD * head + HEAD)
        parts = [(c[0, :, cols], c[1, :, cols], bias) for c in (c0, c1, c2, c3)] + [own[cols, :]]
        top, den, num = absorb(query[cols, :], parts, None, None, None)
        num_ref[cols, :] = num
        stats[head, 0:1, :] = top
        stats[head, 1:2, :] = den


def attend(place, messages, sums, gain, cached, own, bias):
    vmem = pl.BlockSpec(memory_space=pltpu.VMEM)
    return pl.pallas_call(
        attend_kernel,
        in_specs=[pl.BlockSpec(memory_space=pltpu.SMEM)]
        + [pl.BlockSpec(memory_space=pltpu.HBM)] * 4
        + [vmem] * 8,
        out_specs=[vmem] * 3,
        scratch_shapes=[pltpu.VMEM((4, 2 * COLS, HALF_TOK), F32), pltpu.SemaphoreType.DMA((4,))],
        out_shape=[
            jax.ShapeDtypeStruct((PART, HALF_TOK), BF16),
            jax.ShapeDtypeStruct((PART_HEADS, 8, HALF_TOK), F32),
            jax.ShapeDtypeStruct((PART, HALF_TOK), F32),
        ],
        compiler_params=params(20),
        cost_estimate=pl.CostEstimate(flops=700_000_000, bytes_accessed=5_000_000, transcendentals=1_300_000),
        name="attend",
    )(place, *messages, sums, gain, *cached, own, bias)


def close_kernel(place_ref, query, stats_ref, num_ref, near, spread, beside, out_ref, stats):
    stats[...] = jnp.zeros_like(stats)
    first = place_ref[0] == 0

    for h in range(PART_HEADS):
        cols = slice(HEAD * h, HEAD * h + HEAD)
        parts = [
            near[cols, :],
            jnp.where(first, spread[0, cols, :], beside[0, cols, :]),
            jnp.where(first, spread[1, cols, :], beside[1, cols, :]),
        ]
        top, den, num = absorb(
            query[cols, :], parts, stats_ref[h, 0:1, :], stats_ref[h, 1:2, :], num_ref[cols, :]
        )
        out_ref[:, cols] = (num / den).T.astype(BF16)
        stats[h : h + 1, :] = top
        stats[h + 8 : h + 9, :] = den
    full = stats[0:16, :]
    hi = full.astype(BF16).astype(F32)
    mid = (full - hi).astype(BF16).astype(F32)
    stats[0:16, :] = hi
    stats[16:32, :] = mid
    stats[32:48, :] = full - hi - mid
    out_ref[:, PART : PART + 128] = stats[...].T.astype(BF16)


def close(place, query, stats, num, fresh):
    vmem = pl.BlockSpec(memory_space=pltpu.VMEM)
    return pl.pallas_call(
        close_kernel,
        in_specs=[pl.BlockSpec(memory_space=pltpu.SMEM)] + [vmem] * 6,
        out_shape=jax.ShapeDtypeStruct((HALF_TOK, PART + 128), BF16),
        scratch_shapes=[pltpu.VMEM((128, HALF_TOK), F32)],
        compiler_params=params(8),
        name="close",
    )(place, query, stats, num, *fresh)


def finish_kernel(step_ref, in_ref, hidden_ref, mod_ref, out_ref):
    for g in range(8):
        tops, dens = [], []
        for j in range(4):
            parts = in_ref[8 * (g // 2) + 2 * j + g % 2, :, PART : PART + 128].astype(F32)
            full = parts[:, 0:16] + parts[:, 16:32] + parts[:, 32:48]
            tops.append(full[:, 0:8])
            dens.append(full[:, 8:16])
        top = jnp.maximum(jnp.maximum(tops[0], tops[1]), jnp.maximum(tops[2], tops[3]))
        shares = [jnp.exp((t - top) * (1.0 / math.sqrt(HEAD))) * d for t, d in zip(tops, dens)]
        rest = 1.0 / (shares[0] + shares[1] + shares[2] + shares[3])
        shares = [share * rest for share in shares]
        for n in range(PART_HEADS):
            cols = slice(HEAD * n, HEAD * n + HEAD)
            to = slice(PART * g + HEAD * n, PART * g + HEAD * n + HEAD)
            joined = jnp.zeros((TOK, HEAD), F32)
            for j in range(4):
                joined = joined + in_ref[8 * (g // 2) + 2 * j + g % 2, :, cols].astype(F32) * shares[j][:, n : n + 1]
            out_ref[:, to] = (
                hidden_ref[:, to].astype(F32) + mod_ref[0, 2:3, to] * joined
            ).astype(BF16)


def finish(shares, hidden, modulation, step_index):
    return pl.pallas_call(
        finish_kernel,
        grid_spec=pltpu.PrefetchScalarGridSpec(
            num_scalar_prefetch=1,
            grid=(1,),
            in_specs=[
                pl.BlockSpec((32, TOK, PART + 128), lambda i, step: (0, 0, 0)),
                pl.BlockSpec((TOK, WIDTH), lambda i, step: (0, 0)),
                pl.BlockSpec((1, 3, WIDTH), lambda i, step: (step[0], 0, 0)),
            ],
            out_specs=pl.BlockSpec((TOK, WIDTH), lambda i, step: (0, 0)),
        ),
        out_shape=jax.ShapeDtypeStruct((TOK, WIDTH), BF16),
        compiler_params=params(8),
        name="finish",
    )(step_index, shares, hidden, modulation)


def flipped(value, axes, sizes, by):
    count = math.prod(sizes)
    return lax.ppermute(value, axes, [(i, i ^ by) for i in range(count)])


def shards(
    hidden, w_qkv, q_gain, k_gain, modulation, step_index, cache_k, cache_v, slot_rank, visible
):
    zl, core = lax.axis_index("zl"), lax.axis_index("core")
    zh1, half, x_here = lax.axis_index("zh1"), lax.axis_index("zh0"), lax.axis_index("x")
    y_here = lax.axis_index("y")
    fetch = lax.axis_index(SECTION)
    group = lax.axis_index(GROUPS)
    place = jnp.stack([core, half, x_here, zl, y_here, zh1]).astype(jnp.int32)

    moved = [(s, (s + 1) % 4) for s in range(4)]
    mine = lax.ppermute(hidden[0], SECTION, moved)
    other = lax.ppermute(
        hidden[0], SECTION + ("zh1",), [(2 * s + z, 2 * t + 1 - z) for s, t in moved for z in range(2)]
    )
    numbers = lax.ppermute(jnp.concatenate([step_index, visible]), SECTION, moved)

    w_sent = lax.dynamic_slice_in_dim(w_qkv, fetch * TILE, TILE, 2)
    w_sent, mine, other = lax.optimization_barrier((w_sent, mine, other))
    w0 = swapped(w_sent, "zh0")
    pair = modulate(numbers, place, mine, other, modulation)
    row = jnp.concatenate([pair] + [flipped(pair, "x", (4,), i) for i in (1, 2, 3)], axis=0)
    tokens = [flipped(row, "y", (4,), i) for i in (1, 2, 3)]
    w0, cache_k, cache_v, row = lax.optimization_barrier((w0, cache_k, cache_v, row))
    w1 = swapped(w0, "zl")
    w2 = swapped(w0, "core")

    caches = jnp.stack([cache_k, cache_v]).reshape(2, SLOTS * TOK, WIDTH)
    towards = 2 * (y_here ^ fetch)
    c_same = lax.dynamic_slice_in_dim(caches, (towards + zh1) * PART, PART, 2)
    c_flip = lax.dynamic_slice_in_dim(caches, ((towards ^ 4) + 1 - zh1) * PART, PART, 2)
    places = [(f, y, z) for f in range(4) for y in range(4) for z in range(2)]
    spot = lambda f, y, z: 8 * f + 2 * y + z
    four = SECTION + GROUPS
    c_same = lax.ppermute(c_same, four, [(spot(f, y, z), spot(f, y ^ f, z)) for f, y, z in places])
    c_flip = lax.ppermute(
        c_flip, four, [(spot(f ^ 2, y, z), spot(f, y ^ f, 1 - z)) for f, y, z in places]
    )

    new_rank = (slot_rank + 1) % SLOTS
    seen = (slot_rank != SLOTS - 1) & (new_rank < numbers[1])
    bias = jnp.where(seen, 0.0, -jnp.inf).astype(F32)
    bias = jnp.tile(jnp.repeat(bias, TOK), CACHED // (4 * TOK * SLOTS))[:, None]
    q_cols = lax.dynamic_slice_in_dim(q_gain, group * PART, PART)[:, None]
    k_cols = lax.dynamic_slice_in_dim(k_gain, group * PART, PART)[:, None]

    w1, tokens, c_same, c_flip, bias, q_cols, k_cols = lax.optimization_barrier(
        (w1, tokens, c_same, c_flip, bias, q_cols, k_cols)
    )
    w3 = swapped(w1, "core")
    cached = jnp.concatenate([c_same, c_flip], axis=1)
    across = swapped(cached, "zh0")
    tokens = [row] + tokens

    sums, m0, m1, m2, m3 = project(place, tokens, w_qkv, (w0, w1, w2, w3))
    messages = [m0] + [flipped(m, "x", (4,), i) for i, m in ((1, m1), (2, m2), (3, m3))]
    sums, across = lax.optimization_barrier((sums, across))
    cached = jnp.concatenate([cached, across], axis=1)
    sums = lax.all_to_all(sums, ("y", "zh1", "x"), 0, 0, tiled=True)
    beyond = swapped(cached, "zl")
    beside = swapped(cached, "core")
    messages, sums, beyond, beside = lax.optimization_barrier((messages, sums, beyond, beside))
    own = own_rows(place, messages, sums, k_cols)
    near = swapped(own, "zh0")
    low = lax.ppermute(own, SECTION, [(0, 2)])
    high = lax.ppermute(own, SECTION + ("zh0",), [(h, 2 * 2 + 1 - h) for h in range(2)])
    cached = [cached, beyond, beside, swapped(beyond, "core")]
    query, stats, num = attend(place, messages, sums, q_cols, cached, own, bias)
    near, low, high, num = lax.optimization_barrier((near, low, high, num))
    fresh = jnp.where(zl == 0, jnp.stack([own, near]), jnp.stack([low, high]))
    passed = lax.ppermute(fresh, SECTION, [(0, 1), (2, 3)])
    shares = close(place, query, stats, num, [near, fresh, passed])
    shares = shares.reshape(32, TOK, PART + 128)
    shares = lax.all_to_all(shares, ("y", "x", "zh1"), 0, 0, tiled=True)
    return finish(shares, mine, modulation, numbers)[None]


def solution(mesh):
    fine = Mesh(mesh.devices.reshape(SIZES), AXES)
    return jax.shard_map(
        shards,
        mesh=fine,
        in_specs=(
            P(SECTION, SHARD, None),
            P(None, SHARD, None),
            P(),
            P(),
            P(),
            P(SECTION),
            P(None, SHARD, None),
            P(None, SHARD, None),
            P(),
            P(SECTION),
        ),
        out_specs=P(SECTION, SHARD, None),
        check_vma=False,
    )
```

```python
import functools
import math

import jax
import jax.numpy as jnp
from jax import lax
from jax.experimental import pallas as pl
from jax.experimental.pallas import tpu as pltpu
from jax.sharding import Mesh
from jax.sharding import PartitionSpec as P

AXES = ("zl", "core", "y", "zh1", "zh0", "x")
SIZES = (2, 2, 4, 2, 2, 4)
SECTION = ("zl", "core")
SHARD = ("y", "zh1", "zh0", "x")
GROUPS = ("y", "zh1")
MEMBERS = ("zh0", "x")

F32 = jnp.float32
BF16 = jnp.bfloat16
EPS = 1e-6
WIDTH = 5120
HEAD = 128
TOK = 8
SLOTS = 7
COLS = 80
PART = 640
PART_HEADS = 5
HALF_TOK = 256
CACHED = 896
TILE = 1280


def params(mebibytes):
    return pltpu.CompilerParams(vmem_limit_bytes=mebibytes * 1024 * 1024)


def swapped(value, axis):
    return lax.ppermute(value, axis, [(0, 1), (1, 0)])


def around(value, axis, by):
    length = lax.axis_size(axis)
    return lax.ppermute(value, axis, [(i, (i + by) % length) for i in range(length)])


def in_order(index, mine, other, axis=0):
    first = index == 0
    return jnp.concatenate(
        [jnp.where(first, mine, other), jnp.where(first, other, mine)], axis=axis
    )


def modulate_kernel(numbers_ref, place_ref, mine_ref, other_ref, mod_ref, out_ref):
    shift = mod_ref[0, 0:1, :]
    scale = mod_ref[0, 1:2, :]

    def of(ref):
        tokens = ref[...].astype(F32)
        centered = tokens - jnp.mean(tokens, axis=-1, keepdims=True)
        variance = jnp.mean(centered * centered, axis=-1, keepdims=True)
        return centered * lax.rsqrt(variance + EPS) * (1.0 + scale) + shift

    mine, other = of(mine_ref), of(other_ref)
    first = place_ref[5] == 0
    rows = jnp.concatenate(
        [jnp.where(first, mine, other), jnp.where(first, other, mine)], axis=0
    ).astype(BF16)
    out_ref[...] = rows


def modulate(numbers, place, mine, other, modulation):
    return pl.pallas_call(
        modulate_kernel,
        grid_spec=pltpu.PrefetchScalarGridSpec(
            num_scalar_prefetch=2,
            grid=(1,),
            in_specs=[
                pl.BlockSpec((TOK, WIDTH), lambda i, n, p: (0, 0)),
                pl.BlockSpec((TOK, WIDTH), lambda i, n, p: (0, 0)),
                pl.BlockSpec((1, 3, WIDTH), lambda i, n, p: (n[0], 0, 0)),
            ],
            out_specs=pl.BlockSpec((2 * TOK, WIDTH), lambda i, n, p: (0, 0)),
        ),
        out_shape=jax.ShapeDtypeStruct((2 * TOK, WIDTH), BF16),
        compiler_params=params(16),
        name="modulate",
    )(numbers, place, mine, other, modulation)


def project_kernel(
    place_ref, x0_hbm, x1_hbm, x2_hbm, x3_hbm, own_hbm, t0_hbm, t1_hbm, t2_hbm, t3_hbm,
    sums_hbm, m0_hbm, m1_hbm, m2_hbm, m3_hbm,
    x_ref, own_ref, t_ref, acc, m_ref, sums_ref, x_sem, own_sem, t_sem, out_sem,
):
    half = place_ref[1]
    mine = pl.multiple_of(half * 3 * COLS, 16)
    theirs = pl.multiple_of((1 - half) * 3 * COLS, 16)

    x_copies = []
    for j, x_hbm in enumerate((x0_hbm, x1_hbm, x2_hbm, x3_hbm)):
        for i in range(4):
            at = pl.multiple_of(64 * (place_ref[4] ^ j) + 16 * (place_ref[2] ^ i), 16)
            x_copies.append(
                pltpu.make_async_copy(
                    x_hbm.at[pl.ds(16 * i, 16), :], x_ref.at[pl.ds(at, 16), :], x_sem.at[4 * j + i]
                )
            )
    own_copies = [
        pltpu.make_async_copy(own_hbm.at[i], own_ref.at[pl.ds(COLS * i, COLS), :], own_sem.at[i])
        for i in range(3)
    ]
    t_copies = [
        pltpu.make_async_copy(t_hbm, t_ref.at[j], t_sem.at[j])
        for j, t_hbm in enumerate((t0_hbm, t1_hbm, t2_hbm, t3_hbm))
    ]
    for copy in x_copies + own_copies + t_copies:
        copy.start()

    def times(weight, x):
        return lax.dot_general(weight, x, (((1,), (1,)), ((), ())), preferred_element_type=F32)

    for copy in x_copies + own_copies:
        copy.wait()
    acc[pl.ds(mine, 3 * COLS), :] = times(own_ref[...], x_ref[...])
    for copy in t_copies:
        copy.wait()
    for tile in range(4):
        j = 2 * (place_ref[0] ^ (tile % 2)) + (place_ref[3] ^ (tile // 2))
        part = times(t_ref[j].reshape(3 * COLS, TILE), x_ref[:, TILE * tile : TILE * tile + TILE])
        if tile:
            acc[pl.ds(theirs, 3 * COLS), :] += part
        else:
            acc[pl.ds(theirs, 3 * COLS), :] = part

    q, k, v = [
        jnp.concatenate(
            [acc[(3 * e + i) * COLS : (3 * e + i + 1) * COLS, :] for e in range(2)], axis=0
        )
        for i in range(3)
    ]
    for i in range(4):
        m_ref[i, :, 0:HALF_TOK] = q
    lane = lax.broadcasted_iota(jnp.int32, (2 * COLS, 128), 1)
    quarters = []
    for t in range(2):
        kt = k[:, 128 * t : 128 * t + 128]
        vt = v[:, 128 * t : 128 * t + 128]
        quarters.append(jnp.where(lane < 64, kt, pltpu.roll(vt, 64, 1)))
        quarters.append(jnp.where(lane < 64, pltpu.roll(kt, 64, 1), vt))
    for here in range(4):

        @pl.when(place_ref[2] == here)
        def _(here=here):
            for i in range(4):
                m_ref[i, :, HALF_TOK : HALF_TOK + 128] = quarters[here ^ i]

    sub = lax.broadcasted_iota(jnp.int32, (TOK, 128), 0)
    tile = jnp.zeros((TOK, 128), F32)
    for i, part in enumerate((q, k)):
        total = jnp.sum(part * part, axis=0, keepdims=True)
        for t in range(2):
            tile = jnp.where(sub == 2 * i + t, total[:, 128 * t : 128 * t + 128], tile)
    for i in range(32):
        sums_ref[i] = tile
    copies = [
        pltpu.make_async_copy(m_ref.at[i], to, out_sem.at[i])
        for i, to in enumerate((m0_hbm, m1_hbm, m2_hbm, m3_hbm))
    ] + [pltpu.make_async_copy(sums_ref, sums_hbm, out_sem.at[4])]
    for copy in copies:
        copy.start()
    for copy in copies:
        copy.wait()


def project(place, x, own, theirs):
    both = (2 * COLS, HALF_TOK + 128)
    outs = [(32, TOK, 128), both, both, both, both]
    hbm = pl.BlockSpec(memory_space=pltpu.HBM)
    return pl.pallas_call(
        project_kernel,
        in_specs=[pl.BlockSpec(memory_space=pltpu.SMEM)] + [hbm] * 9,
        out_specs=[hbm] * 5,
        scratch_shapes=[
            pltpu.VMEM((HALF_TOK, WIDTH), BF16),
            pltpu.VMEM((3 * COLS, WIDTH), BF16),
            pltpu.VMEM((4, 3, COLS, TILE), BF16),
            pltpu.VMEM((6 * COLS, HALF_TOK), F32),
            pltpu.VMEM((4,) + both, F32),
            pltpu.VMEM((32, TOK, 128), F32),
            pltpu.SemaphoreType.DMA((16,)),
            pltpu.SemaphoreType.DMA((3,)),
            pltpu.SemaphoreType.DMA((4,)),
            pltpu.SemaphoreType.DMA((5,)),
        ],
        out_shape=[jax.ShapeDtypeStruct(shape, F32) for shape in outs],
        compiler_params=params(60),
        name="project",
    )(place, *x, own, *theirs)


def gather_rows(place_ref, pieces, held, sem, rate, gain_ref, out_ref, lanes=None):
    copies = [pltpu.make_async_copy(p, held.at[i], sem.at[i]) for i, p in enumerate(pieces)]
    for copy in copies:
        copy.start()
    for i, copy in enumerate(copies):
        copy.wait()
        for e in range(2):
            at = pl.multiple_of((place_ref[2] ^ i) * COLS + e * (PART // 2), 16)
            raw = held[i, COLS * e : COLS * e + COLS, :]
            rows = raw * rate * gain_ref[pl.ds(at, COLS), :]
            if lanes is not None:
                rows = jnp.where(lanes, rows, raw)
            out_ref[pl.ds(at, COLS), :] = rows.astype(BF16)


def all_rates(sums_ref):
    picked = [sums_ref[g] for g in range(32)]
    while len(picked) > 1:
        picked = [a + b for a, b in zip(picked[0::2], picked[1::2])]
    return lax.rsqrt(picked[0] / WIDTH + EPS)


def own_kernel(place_ref, m0_hbm, m1_hbm, m2_hbm, m3_hbm, sums_ref, gain_ref, out_ref, held, sem):
    rates = all_rates(sums_ref)
    rate = jnp.where(place_ref[2] < 2, rates[2:3, :], rates[3:4, :])
    rate = jnp.broadcast_to(rate, (TOK, 128))
    rate = jnp.where(place_ref[2] % 2 == 0, rate, pltpu.roll(rate, 64, 1))[0:1, :]
    lanes = lax.broadcasted_iota(jnp.int32, (COLS, 128), 1) < 64
    pieces = [m.at[:, pl.ds(HALF_TOK, 128)] for m in (m0_hbm, m1_hbm, m2_hbm, m3_hbm)]
    gather_rows(place_ref, pieces, held, sem, rate, gain_ref, out_ref, lanes)


def own_rows(place, messages, sums, gain):
    vmem = pl.BlockSpec(memory_space=pltpu.VMEM)
    return pl.pallas_call(
        own_kernel,
        in_specs=[pl.BlockSpec(memory_space=pltpu.SMEM)]
        + [pl.BlockSpec(memory_space=pltpu.HBM)] * 4
        + [vmem, vmem],
        out_specs=vmem,
        scratch_shapes=[pltpu.VMEM((4, 2 * COLS, 128), F32), pltpu.SemaphoreType.DMA((4,))],
        out_shape=jax.ShapeDtypeStruct((PART, 128), BF16),
        compiler_params=params(8),
        name="own_rows",
    )(place, *messages, sums, gain)


def absorb(q, parts, top, den, num):
    rate = math.log2(math.e) / math.sqrt(HEAD)
    turned = (((0,), (0,)), ((), ()))
    scores = []
    for part in parts:
        if isinstance(part, tuple):
            scores.append(jnp.dot(part[0], q, preferred_element_type=F32) + part[2])
        else:
            scores.append(lax.dot_general(part, q, turned, preferred_element_type=F32)[0:64])
    new_top = functools.reduce(
        jnp.maximum, [jnp.max(s, axis=0, keepdims=True) for s in scores] + ([] if top is None else [top])
    )
    if top is not None:
        factor = jnp.exp2((top - new_top) * rate)
        den, num = den * factor, num * factor
    else:
        den, num = jnp.zeros(new_top.shape, F32), jnp.zeros(q.shape, F32)
    for s, part in zip(scores, parts):
        w = jnp.exp2((s - new_top) * rate)
        den = den + jnp.sum(w, axis=0, keepdims=True)
        w = w.astype(BF16)
        if isinstance(part, tuple):
            num = num + lax.dot_general(part[1], w, turned, preferred_element_type=F32)
        else:
            w = jnp.concatenate([jnp.zeros_like(w), w], axis=0)
            num = num + jnp.dot(part, w, preferred_element_type=F32)
    return new_top, den, num


def attend_kernel(
    place_ref, m0_hbm, m1_hbm, m2_hbm, m3_hbm, sums_ref, gain_ref, c0, c1, c2, c3, own, bias_ref,
    query, stats, num_ref, held, sem,
):
    rates = all_rates(sums_ref)
    rate = jnp.concatenate([rates[0:1, :], rates[1:2, :]], axis=1)
    pieces = [m.at[:, pl.ds(0, HALF_TOK)] for m in (m0_hbm, m1_hbm, m2_hbm, m3_hbm)]
    gather_rows(place_ref, pieces, held, sem, rate, gain_ref, query)
    bias = bias_ref[...]
    for head in range(PART_HEADS):
        cols = slice(HEAD * head, HEAD * head + HEAD)
        parts = [(c[0, :, cols], c[1, :, cols], bias) for c in (c0, c1, c2, c3)] + [own[cols, :]]
        top, den, num = absorb(query[cols, :], parts, None, None, None)
        num_ref[cols, :] = num
        stats[head, 0:1, :] = top
        stats[head, 1:2, :] = den


def attend(place, messages, sums, gain, cached, own, bias):
    vmem = pl.BlockSpec(memory_space=pltpu.VMEM)
    return pl.pallas_call(
        attend_kernel,
        in_specs=[pl.BlockSpec(memory_space=pltpu.SMEM)]
        + [pl.BlockSpec(memory_space=pltpu.HBM)] * 4
        + [vmem] * 8,
        out_specs=[vmem] * 3,
        scratch_shapes=[pltpu.VMEM((4, 2 * COLS, HALF_TOK), F32), pltpu.SemaphoreType.DMA((4,))],
        out_shape=[
            jax.ShapeDtypeStruct((PART, HALF_TOK), BF16),
            jax.ShapeDtypeStruct((PART_HEADS, 8, HALF_TOK), F32),
            jax.ShapeDtypeStruct((PART, HALF_TOK), F32),
        ],
        compiler_params=params(20),
        cost_estimate=pl.CostEstimate(flops=700_000_000, bytes_accessed=5_000_000, transcendentals=1_300_000),
        name="attend",
    )(place, *messages, sums, gain, *cached, own, bias)


def close_kernel(place_ref, query, stats_ref, num_ref, near, spread, beside, out_ref, stats):
    stats[...] = jnp.zeros_like(stats)
    first = place_ref[0] == 0

    for h in range(PART_HEADS):
        cols = slice(HEAD * h, HEAD * h + HEAD)
        parts = [
            near[cols, :],
            jnp.where(first, spread[0, cols, :], beside[0, cols, :]),
            jnp.where(first, spread[1, cols, :], beside[1, cols, :]),
        ]
        top, den, num = absorb(
            query[cols, :], parts, stats_ref[h, 0:1, :], stats_ref[h, 1:2, :], num_ref[cols, :]
        )
        out_ref[:, cols] = (num / den).T.astype(BF16)
        stats[h : h + 1, :] = top
        stats[h + 8 : h + 9, :] = den
    full = stats[0:16, :]
    hi = full.astype(BF16).astype(F32)
    mid = (full - hi).astype(BF16).astype(F32)
    stats[0:16, :] = hi
    stats[16:32, :] = mid
    stats[32:48, :] = full - hi - mid
    out_ref[:, PART : PART + 128] = stats[...].T.astype(BF16)


def close(place, query, stats, num, fresh):
    vmem = pl.BlockSpec(memory_space=pltpu.VMEM)
    return pl.pallas_call(
        close_kernel,
        in_specs=[pl.BlockSpec(memory_space=pltpu.SMEM)] + [vmem] * 6,
        out_shape=jax.ShapeDtypeStruct((HALF_TOK, PART + 128), BF16),
        scratch_shapes=[pltpu.VMEM((128, HALF_TOK), F32)],
        compiler_params=params(8),
        name="close",
    )(place, query, stats, num, *fresh)


def finish_kernel(step_ref, in_ref, hidden_ref, mod_ref, out_ref):
    for g in range(8):
        tops, dens = [], []
        for j in range(4):
            parts = in_ref[8 * (g // 2) + 2 * j + g % 2, :, PART : PART + 128].astype(F32)
            full = parts[:, 0:16] + parts[:, 16:32] + parts[:, 32:48]
            tops.append(full[:, 0:8])
            dens.append(full[:, 8:16])
        top = jnp.maximum(jnp.maximum(tops[0], tops[1]), jnp.maximum(tops[2], tops[3]))
        shares = [jnp.exp((t - top) * (1.0 / math.sqrt(HEAD))) * d for t, d in zip(tops, dens)]
        rest = 1.0 / (shares[0] + shares[1] + shares[2] + shares[3])
        shares = [share * rest for share in shares]
        for n in range(PART_HEADS):
            cols = slice(HEAD * n, HEAD * n + HEAD)
            to = slice(PART * g + HEAD * n, PART * g + HEAD * n + HEAD)
            joined = jnp.zeros((TOK, HEAD), F32)
            for j in range(4):
                joined = joined + in_ref[8 * (g // 2) + 2 * j + g % 2, :, cols].astype(F32) * shares[j][:, n : n + 1]
            out_ref[:, to] = (
                hidden_ref[:, to].astype(F32) + mod_ref[0, 2:3, to] * joined
            ).astype(BF16)


def finish(shares, hidden, modulation, step_index):
    return pl.pallas_call(
        finish_kernel,
        grid_spec=pltpu.PrefetchScalarGridSpec(
            num_scalar_prefetch=1,
            grid=(1,),
            in_specs=[
                pl.BlockSpec((32, TOK, PART + 128), lambda i, step: (0, 0, 0)),
                pl.BlockSpec((TOK, WIDTH), lambda i, step: (0, 0)),
                pl.BlockSpec((1, 3, WIDTH), lambda i, step: (step[0], 0, 0)),
            ],
            out_specs=pl.BlockSpec((TOK, WIDTH), lambda i, step: (0, 0)),
        ),
        out_shape=jax.ShapeDtypeStruct((TOK, WIDTH), BF16),
        compiler_params=params(8),
        name="finish",
    )(step_index, shares, hidden, modulation)


def flipped(value, axes, sizes, by):
    count = math.prod(sizes)
    return lax.ppermute(value, axes, [(i, i ^ by) for i in range(count)])


def shards(
    hidden, w_qkv, q_gain, k_gain, modulation, step_index, cache_k, cache_v, slot_rank, visible
):
    zl, core = lax.axis_index("zl"), lax.axis_index("core")
    zh1, half, x_here = lax.axis_index("zh1"), lax.axis_index("zh0"), lax.axis_index("x")
    y_here = lax.axis_index("y")
    fetch = lax.axis_index(SECTION)
    group = lax.axis_index(GROUPS)
    place = jnp.stack([core, half, x_here, zl, y_here, zh1]).astype(jnp.int32)

    moved = [(s, (s + 1) % 4) for s in range(4)]
    mine = lax.ppermute(hidden[0], SECTION, moved)
    other = lax.ppermute(
        hidden[0], SECTION + ("zh1",), [(2 * s + z, 2 * t + 1 - z) for s, t in moved for z in range(2)]
    )
    numbers = lax.ppermute(jnp.concatenate([step_index, visible]), SECTION, moved)

    w_sent = lax.dynamic_slice_in_dim(w_qkv, fetch * TILE, TILE, 2)
    w_sent, mine, other = lax.optimization_barrier((w_sent, mine, other))
    w0 = swapped(w_sent, "zh0")
    pair = modulate(numbers, place, mine, other, modulation)
    row = jnp.concatenate([pair] + [flipped(pair, "x", (4,), i) for i in (1, 2, 3)], axis=0)
    tokens = [flipped(row, "y", (4,), i) for i in (1, 2, 3)]
    w0, cache_k, cache_v, row = lax.optimization_barrier((w0, cache_k, cache_v, row))
    w1 = swapped(w0, "zl")
    w2 = swapped(w0, "core")

    caches = jnp.stack([cache_k, cache_v]).reshape(2, SLOTS * TOK, WIDTH)
    towards = 2 * (y_here ^ fetch)
    c_same = lax.dynamic_slice_in_dim(caches, (towards + zh1) * PART, PART, 2)
    c_flip = lax.dynamic_slice_in_dim(caches, ((towards ^ 4) + 1 - zh1) * PART, PART, 2)
    places = [(f, y, z) for f in range(4) for y in range(4) for z in range(2)]
    spot = lambda f, y, z: 8 * f + 2 * y + z
    four = SECTION + GROUPS
    c_same = lax.ppermute(c_same, four, [(spot(f, y, z), spot(f, y ^ f, z)) for f, y, z in places])
    c_flip = lax.ppermute(
        c_flip, four, [(spot(f ^ 2, y, z), spot(f, y ^ f, 1 - z)) for f, y, z in places]
    )

    new_rank = (slot_rank + 1) % SLOTS
    seen = (slot_rank != SLOTS - 1) & (new_rank < numbers[1])
    bias = jnp.where(seen, 0.0, -jnp.inf).astype(F32)
    bias = jnp.tile(jnp.repeat(bias, TOK), CACHED // (4 * TOK * SLOTS))[:, None]
    q_cols = lax.dynamic_slice_in_dim(q_gain, group * PART, PART)[:, None]
    k_cols = lax.dynamic_slice_in_dim(k_gain, group * PART, PART)[:, None]

    w1, tokens, c_same = lax.optimization_barrier((w1, tokens, c_same))
    w3 = swapped(w1, "core")
    w3, c_flip, bias, q_cols, k_cols = lax.optimization_barrier((w3, c_flip, bias, q_cols, k_cols))
    cached = jnp.concatenate([c_same, c_flip], axis=1)
    across = swapped(cached, "zh0")
    tokens = [row] + tokens

    sums, m0, m1, m2, m3 = project(place, tokens, w_qkv, (w0, w1, w2, w3))
    messages = [m0] + [flipped(m, "x", (4,), i) for i, m in ((1, m1), (2, m2), (3, m3))]
    sums, across = lax.optimization_barrier((sums, across))
    cached = jnp.concatenate([cached, across], axis=1)
    sums = lax.all_to_all(sums, ("y", "zh1", "x"), 0, 0, tiled=True)
    beyond = swapped(cached, "zl")
    beside = swapped(cached, "core")
    messages, sums, beyond, beside = lax.optimization_barrier((messages, sums, beyond, beside))
    own = own_rows(place, messages, sums, k_cols)
    near = swapped(own, "zh0")
    low = lax.ppermute(own, SECTION, [(0, 2)])
    high = lax.ppermute(own, SECTION + ("zh0",), [(h, 2 * 2 + 1 - h) for h in range(2)])
    cached = [cached, beyond, beside, swapped(beyond, "core")]
    query, stats, num = attend(place, messages, sums, q_cols, cached, own, bias)
    near, low, high, num = lax.optimization_barrier((near, low, high, num))
    fresh = jnp.where(zl == 0, jnp.stack([own, near]), jnp.stack([low, high]))
    passed = lax.ppermute(fresh, SECTION, [(0, 1), (2, 3)])
    shares = close(place, query, stats, num, [near, fresh, passed])
    shares = shares.reshape(32, TOK, PART + 128)
    shares = lax.all_to_all(shares, ("y", "x", "zh1"), 0, 0, tiled=True)
    return finish(shares, mine, modulation, numbers)[None]


def solution(mesh):
    fine = Mesh(mesh.devices.reshape(SIZES), AXES)
    return jax.shard_map(
        shards,
        mesh=fine,
        in_specs=(
            P(SECTION, SHARD, None),
            P(None, SHARD, None),
            P(),
            P(),
            P(),
            P(SECTION),
            P(None, SHARD, None),
            P(None, SHARD, None),
            P(),
            P(SECTION),
        ),
        out_specs=P(SECTION, SHARD, None),
        check_vma=False,
    )
```
